128 devices in a mesh: kcol: 16 (over y, z_hi, core), ion: 8 (over x, z_lo).
Axes of the slice: x: 4, y: 4, z: 4 (z_hi: 2, z_lo: 2; z = z_hi * 2 + z_lo), core: 2. Of those that a mesh axis runs over, the one named last changes fastest.
Arguments:
- ions: float32 [4, 327680], P(None, ('kcol', 'ion')), may hold values from -1.5 to 1.5, as said below
- col_ids: int32 [2048], P('kcol'), may hold values from 0 to 4095, as said below
Outputs:
- ion_forces: float32 [4, 327680], P(None, ('kcol', 'ion'))
- energy: float32 [], replicated
The draws below stay inside these ranges and needn't reach their ends.
Inputs may be any that keep to these rules, and one draw needn't show every extreme that they name: `col_ids`: distinct column numbers. `ions`: rows 0 to 2 lie in [0, 1); row 3 has magnitudes 0.5 to 1.5.
All inputs are finite; a program needn't handle non-finite values.
Results may differ from the reference program's by a relative error of at most 0.0003.
Values sent between devices are 32-bit elements; how exact they have to be, the bound alone decides.
A program may use at most 64 MiB of HBM per device.

```python
import math
import jax
import jax.numpy as jnp
from jax import lax

KX = 32
ION_DEV = 2560
COLUMNS = 2048
TOTAL_IONS = 327680


def draw_ions(key, part):
    key_pos = jax.random.fold_in(key, 11)
    key_mag = jax.random.fold_in(key, 12)
    key_sign = jax.random.fold_in(key, 13)
    coords = jax.random.uniform(key_pos, (3, TOTAL_IONS), jnp.float32, 0.0, 1.0)
    signs = jnp.where(jax.random.bernoulli(key_sign, 0.5, (TOTAL_IONS,)), 1.0, -1.0).astype(jnp.float32)
    magnitude = jax.random.uniform(key_mag, (TOTAL_IONS,), jnp.float32, 0.5, 1.5)
    charges = signs * magnitude
    return jnp.concatenate([coords, charges[None, :]], 0).astype(jnp.float32)


def draw_col_ids(key, part):
    order = jax.random.permutation(jax.random.fold_in(key, 21), jnp.arange(4096, dtype=jnp.int32))
    return order[:COLUMNS].astype(jnp.int32)


def setup_inputs(seed: int = 0) -> dict:
    keys = jax.random.split(jax.random.key(seed), 3)
    return {
        "ions": draw_ions(jax.random.fold_in(keys[2], 71), 0),
        "col_ids": draw_col_ids(jax.random.fold_in(keys[2], 71), 0),
    }


def wave_numbers(col_ids):
    wave_x = jnp.arange(KX, dtype=jnp.int32)
    wave_y = col_ids // 64 - 32
    wave_z = col_ids % 64 - 32
    return (wave_x, wave_y, wave_z)

def kspace_weight(wave_x, wave_y, wave_z):
    radial = wave_y * wave_y + wave_z * wave_z
    along = wave_x * wave_x
    squared = along[:, None] + radial[None, :]
    inside = (squared <= 1024) & (squared > 0)
    squared_f = squared.astype(jnp.float32)
    halving = jnp.where(wave_x == 0, jnp.float32(0.5), jnp.float32(1.0))[:, None]
    return jnp.where(inside, halving * jnp.exp(-squared_f / 1600.0) / jnp.maximum(squared_f, 1.0), jnp.float32(0.0))

def phase_tables(block, wave_x, wave_y, wave_z):
    two_pi = 2.0 * math.pi
    angle_x = two_pi * wave_x.astype(jnp.float32)[:, None] * block[0][None, :]
    angle_yz = two_pi * (wave_y.astype(jnp.float32)[:, None] * block[1][None, :] + wave_z.astype(jnp.float32)[:, None] * block[2][None, :])
    return (jnp.cos(angle_x), jnp.sin(angle_x), jnp.cos(angle_yz), jnp.sin(angle_yz))

def factor_piece(block, waves):
    cos_x, sin_x, cos_yz, sin_yz = phase_tables(block, *waves)
    charge = block[3][None, :]
    left = jnp.concatenate([charge * cos_x, charge * sin_x], 0)
    right = jnp.concatenate([cos_yz, sin_yz], 0)
    product = lax.dot_general(left, right, (((1,), (1,)), ((), ())), precision=lax.Precision.HIGHEST, preferred_element_type=jnp.float32)
    nwave = cos_x.shape[0]
    ncol = cos_yz.shape[0]
    real_part = product[:nwave, :ncol] - product[nwave:, ncol:]
    imag_part = product[:nwave, ncol:] + product[nwave:, :ncol]
    return jnp.stack([real_part, imag_part])

def combine_matrix(weight, factor, wave_x):
    g_real = weight * factor[0]
    g_imag = -weight * factor[1]
    scaled = wave_x.astype(jnp.float32)[:, None]
    x_real = scaled * g_real
    x_imag = scaled * g_imag
    return jnp.concatenate([jnp.concatenate([g_real.T, -g_imag.T], 1), jnp.concatenate([g_imag.T, g_real.T], 1), jnp.concatenate([x_real.T, -x_imag.T], 1), jnp.concatenate([x_imag.T, x_real.T], 1)], 0)

def force_piece(block, combined, waves, force_scale, potential_scale):
    cos_x, sin_x, cos_yz, sin_yz = phase_tables(block, *waves)
    basis = jnp.concatenate([cos_x, sin_x], 0)
    spread = jnp.dot(combined, basis, precision=lax.Precision.HIGHEST, preferred_element_type=jnp.float32)
    ncol = cos_yz.shape[0]
    h_real0 = spread[:ncol]
    h_imag0 = spread[ncol:2 * ncol]
    h_real1 = spread[2 * ncol:3 * ncol]
    h_imag1 = spread[3 * ncol:]
    imag_zero = h_real0 * sin_yz + h_imag0 * cos_yz
    real_zero = h_real0 * cos_yz - h_imag0 * sin_yz
    imag_one = h_real1 * sin_yz + h_imag1 * cos_yz
    charge = block[3]
    wave_y = waves[1].astype(jnp.float32)[:, None]
    wave_z = waves[2].astype(jnp.float32)[:, None]
    force_x = force_scale * charge * lax.optimization_barrier(jnp.sum(imag_one, 0))
    force_y = force_scale * charge * lax.optimization_barrier(jnp.sum(wave_y * imag_zero, 0))
    force_z = force_scale * charge * lax.optimization_barrier(jnp.sum(wave_z * imag_zero, 0))
    potential = potential_scale * lax.optimization_barrier(jnp.sum(real_zero, 0))
    return jnp.stack([force_x, force_y, force_z, potential])

def reference(ions, col_ids):
    waves = wave_numbers(col_ids)
    weight = kspace_weight(*waves)
    blocks = ions.reshape(4, -1, ION_DEV).transpose(1, 0, 2)

    def add_factor(total, block):
        return (total + factor_piece(block, waves), None)
    factor, unused = lax.scan(add_factor, jnp.zeros((2, KX, COLUMNS), jnp.float32), blocks)
    energy = jnp.float32(0.01 / TOTAL_IONS) * jnp.sum(weight * (factor[0] * factor[0] + factor[1] * factor[1]))
    combined = combine_matrix(weight, factor, waves[0])
    force_scale = jnp.float32(0.04 * math.pi / math.sqrt(TOTAL_IONS))
    potential_scale = jnp.float32(0.4 / math.sqrt(TOTAL_IONS))
    pieces = lax.map(lambda block: force_piece(block, combined, waves, force_scale, potential_scale), blocks)
    ion_forces = pieces.transpose(1, 0, 2).reshape(4, TOTAL_IONS)
    return (ion_forces, energy)
```

```python
import math

import jax
import jax.numpy as jnp
from jax import lax
from jax.experimental import pallas as pl
from jax.experimental.pallas import tpu as pltpu
from jax.sharding import PartitionSpec as P

NA = 512
NB = 512
VMEM_LIMIT = 56 * 1024 * 1024
F32 = jnp.float32
BF16 = jnp.bfloat16
COS = [(-1.0) ** k / math.factorial(2 * k) for k in range(8)]
SIN = [(-1.0) ** k / math.factorial(2 * k + 1) for k in range(7)]


def cos_sin(turns):
    half = jnp.floor(2.0 * turns + 0.5)
    rest = turns - 0.5 * half
    sign = 1.0 - 4.0 * (0.5 * half - jnp.floor(0.5 * half))
    angle = (2.0 * math.pi) * rest
    square = angle * angle
    cosine = jnp.full_like(square, COS[-1])
    for c in COS[-2::-1]:
        cosine = cosine * square + c
    sine = jnp.full_like(square, SIN[-1])
    for c in SIN[-2::-1]:
        sine = sine * square + c
    return cosine * sign, sine * angle * sign


def rows(count, width):
    return lax.broadcasted_iota(jnp.int32, (count, width), 0).astype(F32)


def base_tables(block):
    width = block.shape[1]
    wave = rows(32, width)
    cx, sx = cos_sin(wave * block[0:1])
    cy, sy = cos_sin(wave * block[1:2])
    eight = rows(8, width)
    freq = jnp.where(eight < 4.0, eight + 0.5, 8.0 * eight - 28.5)
    cz, sz = cos_sin(freq * block[2:3])
    return wave, cx, sx, cy, sy, freq, cz, sz


def far_tables(block):
    cy, sy = cos_sin(32.0 * block[1:2])
    cz, sz = cos_sin(32.0 * block[2:3])
    return cy, sy, cz, sz


def split(value):
    high = value.astype(BF16)
    low = (value - high.astype(F32)).astype(BF16)
    return high, low


def build(block, base, a_hi, a_lo, b_hi, b_lo, lanes):
    wave, cx, sx, cy, sy, freq, cz, sz = base
    tx = jnp.concatenate([cx, sx], 0)
    charge = block[3:4]
    for r in range(4):
        for cs, table in enumerate((cz, sz)):
            at = pl.ds(r * 128 + cs * 64, 64)
            high, low = split((charge * table[r : r + 1]) * tx)
            a_hi[at, lanes] = high
            a_lo[at, lanes] = low
    for cs, table in enumerate((cz, sz)):
        for ycs, ty in enumerate((cy, sy)):
            for p in range(4):
                at = pl.ds(cs * 256 + ycs * 128 + p * 32, 32)
                high, low = split(table[4 + p : 5 + p] * ty)
                b_hi[at, lanes] = high
                b_lo[at, lanes] = low


def dot_nt(a, b):
    return lax.dot_general(a, b, (((1,), (1,)), ((), ())), preferred_element_type=F32)


def mask_rows(ids):
    my = lax.shift_right_logical(ids, 6) - 32
    mz = (ids & 63) - 32
    ay, az = jnp.abs(my), jnp.abs(mz)
    low = az & 7
    plus = low >= 4
    r = jnp.where(plus, low - 4, 3 - low)
    row = r * 8 + jnp.where(plus, 0, 4) + jnp.where(my < 0, 2, 0) + jnp.where(mz < 0, 1, 0)
    lane = lax.shift_right_logical(az, 3) * 32 + ay
    row = jnp.where((ay > 31) | (az > 31), -1, row)
    count = ids.shape[1]
    left = (lax.broadcasted_iota(jnp.int32, (32, count), 0) == row).astype(F32).astype(BF16)
    right = (lax.broadcasted_iota(jnp.int32, (128, count), 0) == lane).astype(F32).astype(BF16)
    return dot_nt(left, right)


def factor_kernel(tile, ions_ref, ids_ref, t_ref, extra_ref, a_hi, a_lo, b_hi, b_lo):
    steps = ions_ref.shape[1] // tile
    ids = ids_ref[...]
    extra_ref[0:32] = mask_rows(ids)
    extra_ref[32:40] = jnp.zeros((8, 128), F32)
    extra_ref[36:37] = (ids == 32).astype(F32)
    extra_ref[37:38] = (ids == 2048).astype(F32)
    t_ref[...] = jnp.zeros_like(t_ref)

    @pl.loop(0, steps)
    def _(step):
        lanes = pl.ds(pl.multiple_of(step * tile, tile), tile)
        block = ions_ref[:, lanes]
        build(block, base_tables(block), a_hi, a_lo, b_hi, b_lo, pl.ds(0, tile))
        charge = block[3:4]
        for k, table in enumerate(far_tables(block)):
            value = charge * table
            total = value[:, 0:128]
            for c in range(1, tile // 128):
                total = total + value[:, c * 128 : (c + 1) * 128]
            extra_ref[32 + k : 33 + k] += total
        left = jnp.concatenate([a_hi[...], a_hi[...], a_lo[...]], 1)
        right = jnp.concatenate([b_hi[...], b_lo[...], b_hi[...]], 1)
        t_ref[...] += dot_nt(left, right)


def weights(t_ref, extra_ref, d_ref, hi, lo):
    lane = lax.broadcasted_iota(jnp.int32, (16, 128), 1)
    my = (lane & 31).astype(F32)
    p = lax.shift_right_logical(lane, 5).astype(F32)
    energy = jnp.zeros((16, 128), F32)
    copies = 1.0 / lax.axis_size("ion")
    for r in range(4):
        masks = extra_ref[r * 8 : r * 8 + 8] * copies
        for half in range(2):
            mx = rows(16, 128) + 16.0 * half
            tt = {}
            for zr in range(2):
                for x in range(2):
                    for zp in range(2):
                        for y in range(2):
                            tt[zr, x, zp, y] = t_ref[
                                pl.ds(r * 128 + zr * 64 + x * 32 + half * 16, 16),
                                pl.ds(zp * 256 + y * 128, 128),
                            ]
            dd = {}
            parts = {}
            for sgn in range(2):
                mz = 8.0 * p + (4.0 + r if sgn == 0 else 3.0 - r)
                m2 = mx * mx + my * my + mz * mz
                live = (m2 <= 1024.0) & (m2 > 0.0)
                h = jnp.where(mx == 0.0, 0.5, 1.0)
                w = jnp.where(live, h * jnp.exp(m2 * (-1.0 / 1600.0)) / jnp.maximum(m2, 1.0), 0.0)
                at = sgn * 4
                mpp, mpm, mmp, mmm = (masks[at + k : at + k + 1] for k in range(4))
                ws1, wd1 = w * (mpp + mmm), w * (mpp - mmm)
                ws2, wd2 = w * (mpm + mmp), w * (mpm - mmp)
                s = 1.0 if sgn == 0 else -1.0
                z = {}
                for x in range(2):
                    for y in range(2):
                        z[x, y, 0] = tt[0, x, 0, y] - s * tt[1, x, 1, y]
                        z[x, y, 1] = tt[0, x, 1, y] + s * tt[1, x, 0, y]
                um = [z[x, 0, 0] - z[x, 1, 1] for x in range(2)]
                up = [z[x, 0, 0] + z[x, 1, 1] for x in range(2)]
                vp = [z[x, 1, 0] + z[x, 0, 1] for x in range(2)]
                vm = [z[x, 1, 0] - z[x, 0, 1] for x in range(2)]
                um2 = [ws1 * um[0] - wd1 * vp[1], ws1 * um[1] + wd1 * vp[0]]
                vp2 = [ws1 * vp[0] + wd1 * um[1], ws1 * vp[1] - wd1 * um[0]]
                up2 = [ws2 * up[0] - wd2 * vm[1], ws2 * up[1] + wd2 * vm[0]]
                vm2 = [ws2 * vm[0] + wd2 * up[1], ws2 * vm[1] - wd2 * up[0]]
                for x in range(2):
                    energy += um[x] * um2[x] + vp[x] * vp2[x] + up[x] * up2[x] + vm[x] * vm2[x]
                    parts[sgn, x, 0, 0] = um2[x] + up2[x]
                    parts[sgn, x, 1, 1] = up2[x] - um2[x]
                    parts[sgn, x, 1, 0] = vp2[x] + vm2[x]
                    parts[sgn, x, 0, 1] = vp2[x] - vm2[x]
            for x in range(2):
                for y in range(2):
                    dd[0, x, 0, y] = parts[0, x, y, 0] + parts[1, x, y, 0]
                    dd[1, x, 1, y] = parts[1, x, y, 0] - parts[0, x, y, 0]
                    dd[0, x, 1, y] = parts[0, x, y, 1] + parts[1, x, y, 1]
                    dd[1, x, 0, y] = parts[0, x, y, 1] - parts[1, x, y, 1]
            for (zr, x, zp, y), value in dd.items():
                at = (pl.ds(r * 128 + zr * 64 + x * 32 + half * 16, 16), pl.ds(zp * 256 + y * 128, 128))
                high, low = split(value)
                d_ref[at] = value
                hi[at] = high
                lo[at] = low
    return energy


def force_kernel(tile, total, ions_ref, t_ref, extra_ref, out_ref, energy_ref, d_ref, d_hi, d_lo, dt_hi, dt_lo, a_hi, a_lo, b_hi, b_lo):
    steps = ions_ref.shape[1] // tile
    energy = weights(t_ref, extra_ref, d_ref, d_hi, d_lo)
    for i in range(NA // 128):
        for j in range(NB // 128):
            block = d_ref[i * 128 : (i + 1) * 128, j * 128 : (j + 1) * 128]
            high, low = split(block.T)
            at = (pl.ds(j * 128, 128), pl.ds(i * 128, 128))
            dt_hi[at] = high
            dt_lo[at] = low
    far = jnp.sum(extra_ref[32:40], 1, keepdims=True)
    copies = 1.0 / lax.axis_size("ion")
    far_weight = 0.5 * math.exp(-1024.0 / 1600.0) / 1024.0
    wy = far_weight * copies * far[4:5]
    wz = far_weight * copies * far[5:6]
    fcy, fsy, fcz, fsz = wy * far[0:1], wy * far[1:2], wz * far[2:3], wz * far[3:4]
    energy = jnp.sum(jnp.sum(energy, 1, keepdims=True), 0, keepdims=True)
    energy += fcy * far[0:1] + fsy * far[1:2] + fcz * far[2:3] + fsz * far[3:4]
    energy_ref[...] = (0.01 / total) * energy
    force_scale = 0.04 * math.pi / math.sqrt(total)
    potential_scale = 0.4 / math.sqrt(total)

    @pl.loop(0, steps)
    def _(step):
        lanes = pl.ds(pl.multiple_of(step * tile, tile), tile)
        block = ions_ref[:, lanes]
        base = base_tables(block)
        wave, cx, sx, cy, sy, freq, cz, sz = base
        build(block, base, a_hi, a_lo, b_hi, b_lo, pl.ds(0, tile))
        charge = block[3:4]
        dcz, dsz = -freq * sz, freq * cz
        h_a = jnp.dot(
            jnp.concatenate([d_hi[...], d_hi[...], d_lo[...]], 1),
            jnp.concatenate([b_hi[...], b_lo[...], b_hi[...]], 0),
            preferred_element_type=F32,
        )
        h_b = jnp.dot(
            jnp.concatenate([dt_hi[...], dt_hi[...], dt_lo[...]], 1),
            jnp.concatenate([a_hi[...], a_lo[...], a_hi[...]], 0),
            preferred_element_type=F32,
        )
        v0 = jnp.zeros((64, tile), F32)
        vz = jnp.zeros((64, tile), F32)
        for r in range(4):
            for cs in range(2):
                h = h_a[r * 128 + cs * 64 : r * 128 + cs * 64 + 64]
                v0 += (cz, sz)[cs][r : r + 1] * h
                vz += (dcz, dsz)[cs][r : r + 1] * h
        phi = jnp.sum(cx * v0[:32] + sx * v0[32:], 0, keepdims=True)
        grad_x = jnp.sum(wave * (cx * v0[32:] - sx * v0[:32]), 0, keepdims=True)
        grad_z = jnp.sum(cx * vz[:32] + sx * vz[32:], 0, keepdims=True)
        u0 = [jnp.zeros((32, tile), F32) for _ in range(2)]
        uz = [jnp.zeros((32, tile), F32) for _ in range(2)]
        for cs in range(2):
            for ycs in range(2):
                for p in range(4):
                    at = cs * 256 + ycs * 128 + p * 32
                    h = h_b[at : at + 32]
                    u0[ycs] += (cz, sz)[cs][4 + p : 5 + p] * h
                    uz[ycs] += (dcz, dsz)[cs][4 + p : 5 + p] * h
        fcosy, fsiny, fcosz, fsinz = far_tables(block)
        grad_y = jnp.sum(wave * (cy * u0[1] - sy * u0[0]), 0, keepdims=True)
        grad_zb = jnp.sum(cy * uz[0] + sy * uz[1], 0, keepdims=True)
        phi += fcy * fcosy + fsy * fsiny + fcz * fcosz + fsz * fsinz
        far_y = 32.0 * (fsy * fcosy - fcy * fsiny)
        far_z = 32.0 * (fsz * fcosz - fcz * fsinz)
        out_ref[0:1, lanes] = -force_scale * (charge * grad_x)
        out_ref[1:2, lanes] = -force_scale * (grad_y + charge * far_y)
        out_ref[2:3, lanes] = -force_scale * (grad_zb + charge * (grad_z + far_z))
        out_ref[3:4, lanes] = potential_scale * phi


def tables_scratch(tile):
    return [pltpu.VMEM((NA, tile), BF16)] * 2 + [pltpu.VMEM((NB, tile), BF16)] * 2


def factor_call(ions, ids, tile=512):
    return pl.pallas_call(
        lambda *refs: factor_kernel(tile, *refs),
        out_shape=(jax.ShapeDtypeStruct((NA, NB), F32), jax.ShapeDtypeStruct((40, 128), F32)),
        in_specs=[pl.BlockSpec(memory_space=pltpu.VMEM)] * 2,
        out_specs=[pl.BlockSpec(memory_space=pltpu.VMEM)] * 2,
        scratch_shapes=tables_scratch(tile),
        compiler_params=pltpu.CompilerParams(vmem_limit_bytes=VMEM_LIMIT),
    )(ions, ids)


def force_call(ions, t, extra, total, tile=256):
    return pl.pallas_call(
        lambda *refs: force_kernel(tile, total, *refs),
        out_shape=(jax.ShapeDtypeStruct(ions.shape, F32), jax.ShapeDtypeStruct((1, 1), F32)),
        in_specs=[pl.BlockSpec(memory_space=pltpu.VMEM)] * 3,
        out_specs=[pl.BlockSpec(memory_space=pltpu.VMEM)] * 2,
        scratch_shapes=[pltpu.VMEM((NA, NB), F32)] + [pltpu.VMEM((NA, NB), BF16)] * 4 + tables_scratch(tile),
        compiler_params=pltpu.CompilerParams(vmem_limit_bytes=VMEM_LIMIT),
    )(ions, t, extra)


def per_device(ions, col_ids):
    total = ions.shape[1] * lax.axis_size("kcol") * lax.axis_size("ion")
    t, extra = factor_call(ions, col_ids.reshape(1, -1))
    t, extra = lax.psum((t, extra), ("kcol", "ion"))
    forces, energy = force_call(ions, t, extra, total)
    return forces, energy.reshape(())


def solution(mesh):
    return jax.shard_map(
        per_device,
        mesh=mesh,
        in_specs=(P(None, ("kcol", "ion")), P("kcol")),
        out_specs=(P(None, ("kcol", "ion")), P()),
        check_vma=False,
    )
```

```python
import functools
import math

import jax
import jax.numpy as jnp
from jax import lax
from jax.experimental import pallas as pl
from jax.experimental.pallas import tpu as pltpu
from jax.sharding import PartitionSpec as P

NA = 512
NB = 512
VMEM_LIMIT = 60 * 1024 * 1024
F32 = jnp.float32
BF16 = jnp.bfloat16
COS = [(-1.0) ** k / math.factorial(2 * k) for k in range(8)]
SIN = [(-1.0) ** k / math.factorial(2 * k + 1) for k in range(7)]


def cos_sin(turns):
    half = jnp.floor(2.0 * turns + 0.5)
    rest = turns - 0.5 * half
    sign = 1.0 - 4.0 * (0.5 * half - jnp.floor(0.5 * half))
    angle = (2.0 * math.pi) * rest
    square = angle * angle
    cosine = jnp.full_like(square, COS[-1])
    for c in COS[-2::-1]:
        cosine = cosine * square + c
    sine = jnp.full_like(square, SIN[-1])
    for c in SIN[-2::-1]:
        sine = sine * square + c
    return cosine * sign, sine * angle * sign


def rows(count, width):
    return lax.broadcasted_iota(jnp.int32, (count, width), 0).astype(F32)


def base_tables(block):
    width = block.shape[1]
    wave = rows(32, width)
    cx, sx = cos_sin(wave * block[0:1])
    cy, sy = cos_sin(wave * block[1:2])
    eight = rows(8, width)
    freq = jnp.where(eight < 4.0, eight + 0.5, 8.0 * eight - 28.5)
    cz, sz = cos_sin(freq * block[2:3])
    return wave, cx, sx, cy, sy, freq, cz, sz


def split(value):
    high = value.astype(BF16)
    low = (value - high.astype(F32)).astype(BF16)
    return high, low


def build(block, base, a_hi, a_lo, b_hi, b_lo, lanes):
    wave, cx, sx, cy, sy, freq, cz, sz = base
    tx = jnp.concatenate([cx, sx], 0)
    charge = block[3:4]
    for r in range(4):
        for cs, table in enumerate((cz, sz)):
            at = pl.ds(r * 128 + cs * 64, 64)
            high, low = split((charge * table[r : r + 1]) * tx)
            a_hi[at, lanes] = high
            a_lo[at, lanes] = low
    for cs, table in enumerate((cz, sz)):
        for ycs, ty in enumerate((cy, sy)):
            for p in range(4):
                at = pl.ds(cs * 256 + ycs * 128 + p * 32, 32)
                high, low = split(table[4 + p : 5 + p] * ty)
                b_hi[at, lanes] = high
                b_lo[at, lanes] = low


def dot_nt(a, b):
    return lax.dot_general(a, b, (((1,), (1,)), ((), ())), preferred_element_type=F32)


def mask_rows(ids):
    my = lax.shift_right_logical(ids, 6) - 32
    mz = (ids & 63) - 32
    ay, az = jnp.abs(my), jnp.abs(mz)
    low = az & 7
    plus = low >= 4
    r = jnp.where(plus, low - 4, 3 - low)
    row = r * 8 + jnp.where(plus, 0, 4) + jnp.where(my < 0, 2, 0) + jnp.where(mz < 0, 1, 0)
    lane = lax.shift_right_logical(az, 3) * 32 + ay
    row = jnp.where((ay > 31) | (az > 31), -1, row)
    count = ids.shape[1]
    left = (lax.broadcasted_iota(jnp.int32, (32, count), 0) == row).astype(F32).astype(BF16)
    right = (lax.broadcasted_iota(jnp.int32, (128, count), 0) == lane).astype(F32).astype(BF16)
    return dot_nt(left, right)


def weights(h, t_ref, d_ref, hi, lo):
    lane = lax.broadcasted_iota(jnp.int32, (16, 128), 1)
    my = (lane & 31).astype(F32)
    p = lax.shift_right_logical(lane, 5).astype(F32)
    energy = jnp.zeros((16, 128), F32)
    copies = 1.0 / lax.axis_size("ion")
    for r in (2 * h, 2 * h + 1):
        masks = [
            t_ref[r * 128 + k // 4 * 64 + 32 : r * 128 + k // 4 * 64 + 33, k % 4 * 128 : k % 4 * 128 + 128] * copies
            for k in range(8)
        ]
        for half in range(2):
            mx = rows(16, 128) + 16.0 * half
            tt = {}
            for zr in range(2):
                for x in range(2):
                    for zp in range(2):
                        for y in range(2):
                            tt[zr, x, zp, y] = t_ref[
                                pl.ds(r * 128 + zr * 64 + x * 32 + half * 16, 16),
                                pl.ds(zp * 256 + y * 128, 128),
                            ]
                            if x == 1 and half == 0:
                                tt[zr, x, zp, y] = jnp.where(mx == 0.0, 0.0, tt[zr, x, zp, y])
                            if (r, half, zr, x, zp, y) == (0, 0, 0, 0, 0, 1):
                                tt[zr, x, zp, y] = jnp.where(my == 0.0, 0.0, tt[zr, x, zp, y])
            dd = {}
            parts = {}
            for sgn in range(2):
                mz = 8.0 * p + (4.0 + r if sgn == 0 else 3.0 - r)
                m2 = mx * mx + my * my + mz * mz
                live = (m2 <= 1024.0) & (m2 > 0.0)
                h = jnp.where(mx == 0.0, 0.5, 1.0)
                w = jnp.where(live, h * jnp.exp(m2 * (-1.0 / 1600.0)) / jnp.maximum(m2, 1.0), 0.0)
                at = sgn * 4
                mpp, mpm, mmp, mmm = masks[at : at + 4]
                ws1, wd1 = w * (mpp + mmm), w * (mpp - mmm)
                ws2, wd2 = w * (mpm + mmp), w * (mpm - mmp)
                s = 1.0 if sgn == 0 else -1.0
                z = {}
                for x in range(2):
                    for y in range(2):
                        z[x, y, 0] = tt[0, x, 0, y] - s * tt[1, x, 1, y]
                        z[x, y, 1] = tt[0, x, 1, y] + s * tt[1, x, 0, y]
                um = [z[x, 0, 0] - z[x, 1, 1] for x in range(2)]
                up = [z[x, 0, 0] + z[x, 1, 1] for x in range(2)]
                vp = [z[x, 1, 0] + z[x, 0, 1] for x in range(2)]
                vm = [z[x, 1, 0] - z[x, 0, 1] for x in range(2)]
                um2 = [ws1 * um[0] - wd1 * vp[1], ws1 * um[1] + wd1 * vp[0]]
                vp2 = [ws1 * vp[0] + wd1 * um[1], ws1 * vp[1] - wd1 * um[0]]
                up2 = [ws2 * up[0] - wd2 * vm[1], ws2 * up[1] + wd2 * vm[0]]
                vm2 = [ws2 * vm[0] + wd2 * up[1], ws2 * vm[1] - wd2 * up[0]]
                for x in range(2):
                    energy += um[x] * um2[x] + vp[x] * vp2[x] + up[x] * up2[x] + vm[x] * vm2[x]
                    parts[sgn, x, 0, 0] = um2[x] + up2[x]
                    parts[sgn, x, 1, 1] = up2[x] - um2[x]
                    parts[sgn, x, 1, 0] = vp2[x] + vm2[x]
                    parts[sgn, x, 0, 1] = vp2[x] - vm2[x]
            for x in range(2):
                for y in range(2):
                    dd[0, x, 0, y] = parts[0, x, y, 0] + parts[1, x, y, 0]
                    dd[1, x, 1, y] = parts[1, x, y, 0] - parts[0, x, y, 0]
                    dd[0, x, 1, y] = parts[0, x, y, 1] + parts[1, x, y, 1]
                    dd[1, x, 0, y] = parts[0, x, y, 1] - parts[1, x, y, 1]
            for (zr, x, zp, y), value in dd.items():
                at = (pl.ds(r * 128 + zr * 64 + x * 32 + half * 16, 16), pl.ds(zp * 256 + y * 128, 128))
                high, low = split(value)
                d_ref[at] = value
                hi[at] = high
                lo[at] = low
    return energy


MESH = pl.DeviceIdType.MESH


def place():
    k, i = lax.axis_index("kcol"), lax.axis_index("ion")
    return i >> 1, k >> 2, (k & 2) | (i & 1), k & 1


def device(x, y, z, core):
    return {"kcol": (y << 2) | (z & 2) | core, "ion": (x << 1) | (z & 1)}


def peer(me, step):
    x, y, z, core = me
    return (x + (step >> 4)) & 3, (y + ((step >> 2) & 3)) & 3, (z + (step & 3)) & 3, core


def chip(where):
    return where[0] * 16 + where[1] * 4 + where[2]


def tile_of(index, row0):
    row = pl.multiple_of(row0 + (index >> 2) * 8, 8)
    return pl.ds(row, 8), pl.ds(pl.multiple_of((index & 3) * 128, 128), 128)


def kernel(
    tile,
    tile2,
    total,
    ions_ref,
    ids_ref,
    out_ref,
    energy_ref,
    tx_ref,
    ty_ref,
    tz_ref,
    far_ref,
    acc_ref,
    a_hi,
    a_lo,
    b_hi,
    b_lo,
    t_loc,
    sib,
    own,
    parts,
    red,
    full,
    d_ref,
    d_hi,
    d_lo,
    dt_hi,
    dt_lo,
    sems,
):
    ions = ions_ref.shape[1]
    me = place()
    core = me[3]
    sibling = device(me[0], me[1], me[2], 1 - core)
    barrier = pltpu.get_barrier_semaphore()

    def greet(step, carry):
        pl.semaphore_signal(barrier, inc=1, device_id=device(*peer(me, step)), device_id_type=MESH)
        return carry

    lax.fori_loop(1, 64, greet, 0)
    pl.semaphore_signal(barrier, inc=1, device_id=sibling, device_id_type=MESH)

    def to_sibling(h, k, src, dst):
        return pltpu.make_async_remote_copy(
            src_ref=src,
            dst_ref=dst,
            send_sem=sems.at[h, k],
            recv_sem=sems.at[h, k + 1],
            device_id=sibling,
            device_id_type=MESH,
        )

    def all_bytes(h, k):
        pltpu.make_async_copy(parts.at[h], parts.at[h], sems.at[h, k]).wait()

    wave = rows(32, tile)
    freq = rows(8, tile)
    freq = jnp.where(freq < 4.0, freq + 0.5, 8.0 * freq - 28.5)

    far = jnp.zeros((8, 128), F32)
    for s in range(ions // tile):
        lanes = pl.ds(s * tile, tile)
        block = ions_ref[:, lanes]
        base = base_tables(block)
        _, cx, sx, cy, sy, _, cz, sz = base
        tx_ref[0:32, lanes] = cx
        tx_ref[32:64, lanes] = sx
        ty_ref[0:32, lanes] = cy
        ty_ref[32:64, lanes] = sy
        tz_ref[0:8, lanes] = cz
        tz_ref[8:16, lanes] = sz
        build(block, base, a_hi, a_lo, b_hi, b_lo, lanes)
        turns = 32.0 * block[1:3]
        fc, fs = cos_sin(turns)
        four = jnp.concatenate([fc[0:1], fs[0:1], fc[1:2], fs[1:2]], 0)
        far_ref[0:4, lanes] = four
        value = jnp.concatenate([block[3:4] * four, jnp.zeros((4, tile), F32)], 0)
        for c in range(tile // 128):
            far += value[:, c * 128 : (c + 1) * 128]

    def t_block(h):
        for s in range(ions // tile):
            lanes = pl.ds(s * tile, tile)
            at = pl.ds(h * 256, 256)
            high = a_hi[at, lanes]
            left = jnp.concatenate([high, high, a_lo[at, lanes]], 1)
            right = jnp.concatenate([b_hi[:, lanes], b_lo[:, lanes], b_hi[:, lanes]], 1)
            product = dot_nt(left, right)
            if s == 0:
                t_loc[at] = product
            else:
                t_loc[at] += product

    ids = ids_ref[...]
    masks = mask_rows(ids)

    def patch(h):
        for k in range(16 * h, 16 * h + 16):
            t_loc[64 * (k // 4) + 32 : 64 * (k // 4) + 33, k % 4 * 128 : k % 4 * 128 + 128] = masks[k : k + 1]
        if h == 0:
            row = lax.broadcasted_iota(jnp.int32, (8, 128), 0)
            flags = far
            flags = jnp.where(row == 4, (ids == 32).astype(F32), flags)
            flags = jnp.where(row == 5, (ids == 2048).astype(F32), flags)
            lane = lax.broadcasted_iota(jnp.int32, (8, 128), 1)
            column = jnp.sum(flags, 1, keepdims=True)
            t_loc[0:8, 128:256] = jnp.where(lane == 0, column, t_loc[0:8, 128:256])

    def swap(h):
        theirs = pl.ds(pl.multiple_of(256 * h + 128 * (1 - core), 128), 128)
        return to_sibling(h, 0, t_loc.at[theirs], sib.at[h])

    def scatter(h):
        mine = pl.ds(pl.multiple_of(256 * h + 128 * core, 128), 128)
        own[h] = t_loc[mine] + sib[h]

        def send(step, carry):
            other = peer(me, step)
            r, l = tile_of(chip(other), 0)
            pltpu.make_async_remote_copy(
                src_ref=own.at[h, r, l],
                dst_ref=parts.at[h, step - 1],
                send_sem=sems.at[h, 2],
                recv_sem=sems.at[h, 3],
                device_id=device(*other),
                device_id_type=MESH,
            ).start()
            return carry

        lax.fori_loop(1, 64, send, 0)

    def gather(h):
        all_bytes(h, 3)
        r, l = tile_of(chip(me), 0)
        red[h] = own[h, r, l] + jnp.sum(parts[h], 0)
        where = tile_of(chip(me), 256 * h + 128 * core)
        full[where] = red[h]

        def send(step, carry):
            pltpu.make_async_remote_copy(
                src_ref=red.at[h],
                dst_ref=full.at[where],
                send_sem=sems.at[h, 4],
                recv_sem=sems.at[h, 5],
                device_id=device(*peer(me, step)),
                device_id_type=MESH,
            ).start()
            return carry

        lax.fori_loop(1, 64, send, 0)

    def forward(h):
        mine = full.at[pl.ds(pl.multiple_of(256 * h + 128 * core, 128), 128)]
        return to_sibling(h, 6, mine, mine)

    def transpose(h):
        for i in (2 * h, 2 * h + 1):
            for j in range(NB // 128):
                block = d_ref[i * 128 : (i + 1) * 128, j * 128 : (j + 1) * 128]
                high, low = split(block.T)
                at = (pl.ds(j * 128, 128), pl.ds(i * 128, 128))
                dt_hi[at] = high
                dt_lo[at] = low

    def z_rows(lanes, k):
        cz, sz = tz_ref[k : k + 1, lanes], tz_ref[8 + k : 9 + k, lanes]
        f = k + 0.5 if k < 4 else 8.0 * k - 28.5
        return (cz, sz), (-f * sz, f * cz)

    def force_a(h, lanes):
        at = pl.ds(h * 256, 256)
        high = d_hi[at]
        h_a = jnp.dot(
            jnp.concatenate([high, high, d_lo[at]], 1),
            jnp.concatenate([b_hi[:, lanes], b_lo[:, lanes], b_hi[:, lanes]], 0),
            preferred_element_type=F32,
        )
        v0 = vz = None
        for k in range(2):
            z, dz = z_rows(lanes, 2 * h + k)
            for cs in range(2):
                part = h_a[k * 128 + cs * 64 : k * 128 + cs * 64 + 64]
                v0 = z[cs] * part if v0 is None else v0 + z[cs] * part
                vz = dz[cs] * part if vz is None else vz + dz[cs] * part
        cx, sx = tx_ref[0:32, lanes], tx_ref[32:64, lanes]
        n = rows(32, tile2)
        phi = jnp.sum(cx * v0[:32] + sx * v0[32:], 0, keepdims=True)
        grad_x = jnp.sum(n * (cx * v0[32:] - sx * v0[:32]), 0, keepdims=True)
        grad_z = jnp.sum(cx * vz[:32] + sx * vz[32:], 0, keepdims=True)
        return phi, grad_x, grad_z

    def force_b(lanes):
        h_b = jnp.dot(
            jnp.concatenate([dt_hi[...], dt_hi[...], dt_lo[...]], 1),
            jnp.concatenate([a_hi[:, lanes], a_lo[:, lanes], a_hi[:, lanes]], 0),
            preferred_element_type=F32,
        )
        u0, uz = [None, None], [None, None]
        for p in range(4):
            z, dz = z_rows(lanes, 4 + p)
            for cs in range(2):
                for ycs in range(2):
                    at = cs * 256 + ycs * 128 + p * 32
                    part = h_b[at : at + 32]
                    u0[ycs] = z[cs] * part if u0[ycs] is None else u0[ycs] + z[cs] * part
                    uz[ycs] = dz[cs] * part if uz[ycs] is None else uz[ycs] + dz[cs] * part
        cy, sy = ty_ref[0:32, lanes], ty_ref[32:64, lanes]
        n = rows(32, tile2)
        grad_y = jnp.sum(n * (cy * u0[1] - sy * u0[0]), 0, keepdims=True)
        grad_z = jnp.sum(cy * uz[0] + sy * uz[1], 0, keepdims=True)
        return grad_y, grad_z

    t_block(0)
    patch(0)
    pl.semaphore_wait(barrier, 64)
    swap0 = swap(0)
    swap0.start()
    t_block(1)
    patch(1)
    swap1 = swap(1)
    swap1.start()
    swap0.wait_recv()
    scatter(0)
    swap1.wait_recv()
    scatter(1)
    gather(0)
    gather(1)
    all_bytes(0, 5)
    forward0 = forward(0)
    forward0.start()
    forward0.wait_recv()
    energy = weights(0, full, d_ref, d_hi, d_lo)
    transpose(0)

    @pl.loop(0, ions // tile2)
    def _(step):
        lanes = pl.ds(pl.multiple_of(step * tile2, tile2), tile2)
        for k, value in enumerate(force_a(0, lanes)):
            acc_ref[k : k + 1, lanes] = value

    all_bytes(1, 5)
    forward1 = forward(1)
    forward1.start()
    forward1.wait_recv()
    energy += weights(1, full, d_ref, d_hi, d_lo)
    transpose(1)

    copies = 1.0 / lax.axis_size("ion")
    column = full[0:8, 128:129]
    far_weight = 0.5 * math.exp(-1024.0 / 1600.0) / 1024.0
    wy = far_weight * copies * column[4:5]
    wz = far_weight * copies * column[5:6]
    fcy, fsy, fcz, fsz = wy * column[0:1], wy * column[1:2], wz * column[2:3], wz * column[3:4]
    energy = jnp.sum(jnp.sum(energy, 1, keepdims=True), 0, keepdims=True)
    energy += fcy * column[0:1] + fsy * column[1:2] + fcz * column[2:3] + fsz * column[3:4]
    energy_ref[...] = (0.01 / total) * energy
    force_scale = 0.04 * math.pi / math.sqrt(total)
    potential_scale = 0.4 / math.sqrt(total)

    @pl.loop(0, ions // tile2)
    def _(step):
        lanes = pl.ds(pl.multiple_of(step * tile2, tile2), tile2)
        phi, grad_x, grad_z = force_a(1, lanes)
        phi += acc_ref[0:1, lanes]
        grad_x += acc_ref[1:2, lanes]
        grad_z += acc_ref[2:3, lanes]
        grad_y, grad_zb = force_b(lanes)
        charge = ions_ref[3:4, lanes]
        fcosy, fsiny, fcosz, fsinz = (far_ref[k : k + 1, lanes] for k in range(4))
        phi += fcy * fcosy + fsy * fsiny + fcz * fcosz + fsz * fsinz
        far_y = 32.0 * (fsy * fcosy - fcy * fsiny)
        far_z = 32.0 * (fsz * fcosz - fcz * fsinz)
        out_ref[0:1, lanes] = -force_scale * (charge * grad_x)
        out_ref[1:2, lanes] = -force_scale * (grad_y + charge * far_y)
        out_ref[2:3, lanes] = -force_scale * (grad_zb + charge * (grad_z + far_z))
        out_ref[3:4, lanes] = potential_scale * phi

    for h, (first, second) in enumerate(((swap0, forward0), (swap1, forward1))):
        first.wait_send()
        all_bytes(h, 2)
        all_bytes(h, 4)
        second.wait_send()


def per_device(ions, col_ids):
    count = ions.shape[1]
    total = count * lax.axis_size("kcol") * lax.axis_size("ion")
    forces, energy = pl.pallas_call(
        functools.partial(kernel, 512, 256, total),
        out_shape=(jax.ShapeDtypeStruct(ions.shape, F32), jax.ShapeDtypeStruct((1, 1), F32)),
        in_specs=[pl.BlockSpec(memory_space=pltpu.VMEM)] * 2,
        out_specs=[pl.BlockSpec(memory_space=pltpu.VMEM)] * 2,
        scratch_shapes=[
            pltpu.VMEM((64, count), F32),
            pltpu.VMEM((64, count), F32),
            pltpu.VMEM((16, count), F32),
            pltpu.VMEM((8, count), F32),
            pltpu.VMEM((8, count), F32),
            pltpu.VMEM((NA, count), BF16),
            pltpu.VMEM((NA, count), BF16),
            pltpu.VMEM((NB, count), BF16),
            pltpu.VMEM((NB, count), BF16),
            pltpu.VMEM((NA, NB), F32),
            pltpu.VMEM((2, 128, NB), F32),
            pltpu.VMEM((2, 128, NB), F32),
            pltpu.VMEM((2, 63, 8, 128), F32),
            pltpu.VMEM((2, 8, 128), F32),
            pltpu.VMEM((NA, NB), F32),
            pltpu.VMEM((NA, NB), F32),
            pltpu.VMEM((NA, NB), BF16),
            pltpu.VMEM((NA, NB), BF16),
            pltpu.VMEM((NB, NA), BF16),
            pltpu.VMEM((NB, NA), BF16),
            pltpu.SemaphoreType.DMA((2, 8)),
        ],
        compiler_params=pltpu.CompilerParams(
            collective_id=0, has_side_effects=True, vmem_limit_bytes=VMEM_LIMIT
        ),
    )(ions, col_ids.reshape(1, -1))
    return forces, energy.reshape(())


def solution(mesh):
    return jax.shard_map(
        per_device,
        mesh=mesh,
        in_specs=(P(None, ("kcol", "ion")), P("kcol")),
        out_specs=(P(None, ("kcol", "ion")), P()),
        check_vma=False,
    )
```

```python
import functools
import math

import jax
import jax.numpy as jnp
from jax import lax
from jax.experimental import pallas as pl
from jax.experimental.pallas import tpu as pltpu
from jax.sharding import PartitionSpec as P

NA = 512
NB = 512
VMEM_LIMIT = 60 * 1024 * 1024
CUT = 3
LATE = 3
F32 = jnp.float32
BF16 = jnp.bfloat16
COS = [(-1.0) ** k / math.factorial(2 * k) for k in range(8)]
SIN = [(-1.0) ** k / math.factorial(2 * k + 1) for k in range(7)]


def cos_sin(turns):
    half = jnp.floor(2.0 * turns + 0.5)
    rest = turns - 0.5 * half
    sign = 1.0 - 4.0 * (0.5 * half - jnp.floor(0.5 * half))
    angle = (2.0 * math.pi) * rest
    square = angle * angle
    cosine = jnp.full_like(square, COS[-1])
    for c in COS[-2::-1]:
        cosine = cosine * square + c
    sine = jnp.full_like(square, SIN[-1])
    for c in SIN[-2::-1]:
        sine = sine * square + c
    return cosine * sign, sine * angle * sign


def rows(count, width):
    return lax.broadcasted_iota(jnp.int32, (count, width), 0).astype(F32)


def base_tables(block):
    width = block.shape[1]
    wave = rows(32, width)
    cx, sx = cos_sin(wave * block[0:1])
    cy, sy = cos_sin(wave * block[1:2])
    eight = rows(8, width)
    freq = jnp.where(eight < 4.0, eight + 0.5, 8.0 * eight - 28.5)
    cz, sz = cos_sin(freq * block[2:3])
    return wave, cx, sx, cy, sy, freq, cz, sz


def split(value):
    high = value.astype(BF16)
    low = (value - high.astype(F32)).astype(BF16)
    return high, low


def build(block, base, a_hi, a_lo, b_hi, b_lo, lanes):
    wave, cx, sx, cy, sy, freq, cz, sz = base
    tx = jnp.concatenate([cx, sx], 0)
    charge = block[3:4]
    for r in range(4):
        for cs, table in enumerate((cz, sz)):
            at = pl.ds(r * 128 + cs * 64, 64)
            high, low = split((charge * table[r : r + 1]) * tx)
            a_hi[at, lanes] = high
            a_lo[at, lanes] = low
    for cs, table in enumerate((cz, sz)):
        for ycs, ty in enumerate((cy, sy)):
            for p in range(4):
                at = pl.ds(cs * 256 + ycs * 128 + p * 32, 32)
                high, low = split(table[4 + p : 5 + p] * ty)
                b_hi[at, lanes] = high
                b_lo[at, lanes] = low


def dot_nt(a, b):
    return lax.dot_general(a, b, (((1,), (1,)), ((), ())), preferred_element_type=F32)


def mask_rows(ids):
    my = lax.shift_right_logical(ids, 6) - 32
    mz = (ids & 63) - 32
    ay, az = jnp.abs(my), jnp.abs(mz)
    low = az & 7
    plus = low >= 4
    r = jnp.where(plus, low - 4, 3 - low)
    row = r * 8 + jnp.where(plus, 0, 4) + jnp.where(my < 0, 2, 0) + jnp.where(mz < 0, 1, 0)
    lane = lax.shift_right_logical(az, 3) * 32 + ay
    row = jnp.where((ay > 31) | (az > 31), -1, row)
    count = ids.shape[1]
    left = (lax.broadcasted_iota(jnp.int32, (32, count), 0) == row).astype(F32).astype(BF16)
    right = (lax.broadcasted_iota(jnp.int32, (128, count), 0) == lane).astype(F32).astype(BF16)
    return dot_nt(left, right)


def weights(h, t_ref, d_ref, hi, lo):
    lane = lax.broadcasted_iota(jnp.int32, (16, 128), 1)
    my = (lane & 31).astype(F32)
    p = lax.shift_right_logical(lane, 5).astype(F32)
    energy = jnp.zeros((16, 128), F32)
    copies = 1.0 / lax.axis_size("ion")
    for r in (2 * h, 2 * h + 1):
        masks = [
            t_ref[r * 128 + k // 4 * 64 + 32 : r * 128 + k // 4 * 64 + 33, k % 4 * 128 : k % 4 * 128 + 128] * copies
            for k in range(8)
        ]
        for half in range(2):
            mx = rows(16, 128) + 16.0 * half
            tt = {}
            for zr in range(2):
                for x in range(2):
                    for zp in range(2):
                        for y in range(2):
                            tt[zr, x, zp, y] = t_ref[
                                pl.ds(r * 128 + zr * 64 + x * 32 + half * 16, 16),
                                pl.ds(zp * 256 + y * 128, 128),
                            ]
                            if x == 1 and half == 0:
                                tt[zr, x, zp, y] = jnp.where(mx == 0.0, 0.0, tt[zr, x, zp, y])
                            if (r, half, zr, x, zp, y) == (0, 0, 0, 0, 0, 1):
                                tt[zr, x, zp, y] = jnp.where(my == 0.0, 0.0, tt[zr, x, zp, y])
            dd = {}
            parts = {}
            for sgn in range(2):
                mz = 8.0 * p + (4.0 + r if sgn == 0 else 3.0 - r)
                m2 = mx * mx + my * my + mz * mz
                live = (m2 <= 1024.0) & (m2 > 0.0)
                h = jnp.where(mx == 0.0, 0.5, 1.0)
                w = jnp.where(live, h * jnp.exp(m2 * (-1.0 / 1600.0)) / jnp.maximum(m2, 1.0), 0.0)
                at = sgn * 4
                mpp, mpm, mmp, mmm = masks[at : at + 4]
                ws1, wd1 = w * (mpp + mmm), w * (mpp - mmm)
                ws2, wd2 = w * (mpm + mmp), w * (mpm - mmp)
                s = 1.0 if sgn == 0 else -1.0
                z = {}
                for x in range(2):
                    for y in range(2):
                        z[x, y, 0] = tt[0, x, 0, y] - s * tt[1, x, 1, y]
                        z[x, y, 1] = tt[0, x, 1, y] + s * tt[1, x, 0, y]
                um = [z[x, 0, 0] - z[x, 1, 1] for x in range(2)]
                up = [z[x, 0, 0] + z[x, 1, 1] for x in range(2)]
                vp = [z[x, 1, 0] + z[x, 0, 1] for x in range(2)]
                vm = [z[x, 1, 0] - z[x, 0, 1] for x in range(2)]
                um2 = [ws1 * um[0] - wd1 * vp[1], ws1 * um[1] + wd1 * vp[0]]
                vp2 = [ws1 * vp[0] + wd1 * um[1], ws1 * vp[1] - wd1 * um[0]]
                up2 = [ws2 * up[0] - wd2 * vm[1], ws2 * up[1] + wd2 * vm[0]]
                vm2 = [ws2 * vm[0] + wd2 * up[1], ws2 * vm[1] - wd2 * up[0]]
                for x in range(2):
                    energy += um[x] * um2[x] + vp[x] * vp2[x] + up[x] * up2[x] + vm[x] * vm2[x]
                    parts[sgn, x, 0, 0] = um2[x] + up2[x]
                    parts[sgn, x, 1, 1] = up2[x] - um2[x]
                    parts[sgn, x, 1, 0] = vp2[x] + vm2[x]
                    parts[sgn, x, 0, 1] = vp2[x] - vm2[x]
            for x in range(2):
                for y in range(2):
                    dd[0, x, 0, y] = parts[0, x, y, 0] + parts[1, x, y, 0]
                    dd[1, x, 1, y] = parts[1, x, y, 0] - parts[0, x, y, 0]
                    dd[0, x, 1, y] = parts[0, x, y, 1] + parts[1, x, y, 1]
                    dd[1, x, 0, y] = parts[0, x, y, 1] - parts[1, x, y, 1]
            for (zr, x, zp, y), value in dd.items():
                at = (pl.ds(r * 128 + zr * 64 + x * 32 + half * 16, 16), pl.ds(zp * 256 + y * 128, 128))
                high, low = split(value)
                d_ref[at] = value
                hi[at] = high
                lo[at] = low
    return energy


MESH = pl.DeviceIdType.MESH


def hops(step):
    return sum(min(d, 4 - d) for d in (step >> 4, (step >> 2) & 3, step & 3))


ORDER = sorted(range(1, 64), key=lambda step: -hops(step))


def place():
    k, i = lax.axis_index("kcol"), lax.axis_index("ion")
    return i >> 1, k >> 2, (k & 2) | (i & 1), k & 1


def device(x, y, z, core):
    return {"kcol": (y << 2) | (z & 2) | core, "ion": (x << 1) | (z & 1)}


def peer(me, step):
    x, y, z, core = me
    return (x + (step >> 4)) & 3, (y + ((step >> 2) & 3)) & 3, (z + (step & 3)) & 3, core


def chip(where):
    return where[0] * 16 + where[1] * 4 + where[2]


def tile_of(index, row0):
    row = pl.multiple_of(row0 + (index >> 2) * 8, 8)
    return pl.ds(row, 8), pl.ds(pl.multiple_of((index & 3) * 128, 128), 128)


def kernel(
    tile,
    tile2,
    total,
    ions_ref,
    ids_ref,
    out_ref,
    energy_ref,
    tx_ref,
    ty_ref,
    tz_ref,
    far_ref,
    acc_ref,
    a_hi,
    a_lo,
    b_hi,
    b_lo,
    t_loc,
    sib,
    own,
    parts,
    red,
    full,
    d_ref,
    d_hi,
    d_lo,
    dt_hi,
    dt_lo,
    sems,
):
    ions = ions_ref.shape[1]
    me = place()
    core = me[3]
    sibling = device(me[0], me[1], me[2], 1 - core)
    barrier = pltpu.get_barrier_semaphore()

    for step in ORDER:
        pl.semaphore_signal(barrier, inc=1, device_id=device(*peer(me, step)), device_id_type=MESH)
    pl.semaphore_signal(barrier, inc=1, device_id=sibling, device_id_type=MESH)

    def to_sibling(h, k, src, dst):
        return pltpu.make_async_remote_copy(
            src_ref=src,
            dst_ref=dst,
            send_sem=sems.at[h, k],
            recv_sem=sems.at[h, k + 1],
            device_id=sibling,
            device_id_type=MESH,
        )

    def all_bytes(h, k):
        pltpu.make_async_copy(parts.at[h], parts.at[h], sems.at[h, k]).wait()

    wave = rows(32, tile)
    freq = rows(8, tile)
    freq = jnp.where(freq < 4.0, freq + 0.5, 8.0 * freq - 28.5)

    far = jnp.zeros((8, 128), F32)
    for s in range(ions // tile):
        lanes = pl.ds(s * tile, tile)
        block = ions_ref[:, lanes]
        base = base_tables(block)
        _, cx, sx, cy, sy, _, cz, sz = base
        tx_ref[0:32, lanes] = cx
        tx_ref[32:64, lanes] = sx
        ty_ref[0:32, lanes] = cy
        ty_ref[32:64, lanes] = sy
        tz_ref[0:8, lanes] = cz
        tz_ref[8:16, lanes] = sz
        build(block, base, a_hi, a_lo, b_hi, b_lo, lanes)
        turns = 32.0 * block[1:3]
        fc, fs = cos_sin(turns)
        four = jnp.concatenate([fc[0:1], fs[0:1], fc[1:2], fs[1:2]], 0)
        far_ref[0:4, lanes] = four
        value = jnp.concatenate([block[3:4] * four, jnp.zeros((4, tile), F32)], 0)
        for c in range(tile // 128):
            far += value[:, c * 128 : (c + 1) * 128]

    def t_block(h, first, last):
        for s in range(first, last):
            lanes = pl.ds(s * tile, tile)
            at = pl.ds(h * 256, 256)
            high = a_hi[at, lanes]
            left = jnp.concatenate([high, high, a_lo[at, lanes]], 1)
            right = jnp.concatenate([b_hi[:, lanes], b_lo[:, lanes], b_hi[:, lanes]], 1)
            product = dot_nt(left, right)
            if s == 0:
                t_loc[at] = product
            else:
                t_loc[at] += product

    ids = ids_ref[...]
    masks = mask_rows(ids)

    def patch(h):
        for k in range(16 * h, 16 * h + 16):
            t_loc[64 * (k // 4) + 32 : 64 * (k // 4) + 33, k % 4 * 128 : k % 4 * 128 + 128] = masks[k : k + 1]
        if h == 0:
            row = lax.broadcasted_iota(jnp.int32, (8, 128), 0)
            flags = far
            flags = jnp.where(row == 4, (ids == 32).astype(F32), flags)
            flags = jnp.where(row == 5, (ids == 2048).astype(F32), flags)
            lane = lax.broadcasted_iota(jnp.int32, (8, 128), 1)
            column = jnp.sum(flags, 1, keepdims=True)
            t_loc[0:8, 128:256] = jnp.where(lane == 0, column, t_loc[0:8, 128:256])

    def swap(h):
        theirs = pl.ds(pl.multiple_of(256 * h + 128 * (1 - core), 128), 128)
        return to_sibling(h, 0, t_loc.at[theirs], sib.at[h])

    def scatter(h):
        mine = pl.ds(pl.multiple_of(256 * h + 128 * core, 128), 128)
        own[h] = t_loc[mine] + sib[h]

        for step in ORDER:
            other = peer(me, step)
            r, l = tile_of(chip(other), 0)
            pltpu.make_async_remote_copy(
                src_ref=own.at[h, r, l],
                dst_ref=parts.at[h, step - 1],
                send_sem=sems.at[h, 2],
                recv_sem=sems.at[h, 3],
                device_id=device(*other),
                device_id_type=MESH,
            ).start()

    def gather(h):
        all_bytes(h, 3)
        r, l = tile_of(chip(me), 0)
        red[h] = own[h, r, l] + jnp.sum(parts[h], 0)
        where = tile_of(chip(me), 256 * h + 128 * core)
        full[where] = red[h]

        for step in ORDER:
            pltpu.make_async_remote_copy(
                src_ref=red.at[h],
                dst_ref=full.at[where],
                send_sem=sems.at[h, 4],
                recv_sem=sems.at[h, 5],
                device_id=device(*peer(me, step)),
                device_id_type=MESH,
            ).start()

    def forward(h):
        mine = full.at[pl.ds(pl.multiple_of(256 * h + 128 * core, 128), 128)]
        return to_sibling(h, 6, mine, mine)

    def transpose(h):
        for i in (2 * h, 2 * h + 1):
            for j in range(NB // 128):
                block = d_ref[i * 128 : (i + 1) * 128, j * 128 : (j + 1) * 128]
                high, low = split(block.T)
                at = (pl.ds(j * 128, 128), pl.ds(i * 128, 128))
                dt_hi[at] = high
                dt_lo[at] = low

    def z_rows(lanes, k):
        cz, sz = tz_ref[k : k + 1, lanes], tz_ref[8 + k : 9 + k, lanes]
        f = k + 0.5 if k < 4 else 8.0 * k - 28.5
        return (cz, sz), (-f * sz, f * cz)

    def force_a(h, lanes):
        at = pl.ds(h * 256, 256)
        high = d_hi[at]
        h_a = jnp.dot(
            jnp.concatenate([high, high, d_lo[at]], 1),
            jnp.concatenate([b_hi[:, lanes], b_lo[:, lanes], b_hi[:, lanes]], 0),
            preferred_element_type=F32,
        )
        v0 = vz = None
        for k in range(2):
            z, dz = z_rows(lanes, 2 * h + k)
            for cs in range(2):
                part = h_a[k * 128 + cs * 64 : k * 128 + cs * 64 + 64]
                v0 = z[cs] * part if v0 is None else v0 + z[cs] * part
                vz = dz[cs] * part if vz is None else vz + dz[cs] * part
        cx, sx = tx_ref[0:32, lanes], tx_ref[32:64, lanes]
        n = rows(32, tile2)
        phi = jnp.sum(cx * v0[:32] + sx * v0[32:], 0, keepdims=True)
        grad_x = jnp.sum(n * (cx * v0[32:] - sx * v0[:32]), 0, keepdims=True)
        grad_z = jnp.sum(cx * vz[:32] + sx * vz[32:], 0, keepdims=True)
        return phi, grad_x, grad_z

    def force_b(h, lanes):
        at = pl.ds(h * 256, 256)
        high, high_a = dt_hi[:, at], a_hi[at, lanes]
        h_b = jnp.dot(
            jnp.concatenate([high, high, dt_lo[:, at]], 1),
            jnp.concatenate([high_a, a_lo[at, lanes], high_a], 0),
            preferred_element_type=F32,
        )
        u0, uz = [None, None], [None, None]
        for p in range(4):
            z, dz = z_rows(lanes, 4 + p)
            for cs in range(2):
                for ycs in range(2):
                    at = cs * 256 + ycs * 128 + p * 32
                    part = h_b[at : at + 32]
                    u0[ycs] = z[cs] * part if u0[ycs] is None else u0[ycs] + z[cs] * part
                    uz[ycs] = dz[cs] * part if uz[ycs] is None else uz[ycs] + dz[cs] * part
        cy, sy = ty_ref[0:32, lanes], ty_ref[32:64, lanes]
        n = rows(32, tile2)
        grad_y = jnp.sum(n * (cy * u0[1] - sy * u0[0]), 0, keepdims=True)
        grad_z = jnp.sum(cy * uz[0] + sy * uz[1], 0, keepdims=True)
        return grad_y, grad_z

    steps = ions // tile
    t_block(0, 0, steps)
    patch(0)
    pl.semaphore_wait(barrier, 64)
    swap0 = swap(0)
    swap0.start()
    t_block(1, 0, CUT)
    swap0.wait_recv()
    scatter(0)
    t_block(1, CUT, steps)
    patch(1)
    swap1 = swap(1)
    swap1.start()
    swap1.wait_recv()
    scatter(1)
    gather(0)
    gather(1)
    all_bytes(0, 5)
    forward0 = forward(0)
    forward0.start()
    forward0.wait_recv()
    energy = weights(0, full, d_ref, d_hi, d_lo)
    transpose(0)
    forward1 = forward(1)
    steps2 = ions // tile2
    for s in range(steps2):
        lanes = pl.ds(s * tile2, tile2)
        if s == steps2 - LATE:
            all_bytes(1, 5)
            forward1.start()
        for k, value in enumerate(force_a(0, lanes) + force_b(0, lanes)):
            acc_ref[k : k + 1, lanes] = value
    forward1.wait_recv()
    energy += weights(1, full, d_ref, d_hi, d_lo)
    transpose(1)

    copies = 1.0 / lax.axis_size("ion")
    column = full[0:8, 128:129]
    far_weight = 0.5 * math.exp(-1024.0 / 1600.0) / 1024.0
    wy = far_weight * copies * column[4:5]
    wz = far_weight * copies * column[5:6]
    fcy, fsy, fcz, fsz = wy * column[0:1], wy * column[1:2], wz * column[2:3], wz * column[3:4]
    energy = jnp.sum(jnp.sum(energy, 1, keepdims=True), 0, keepdims=True)
    energy += fcy * column[0:1] + fsy * column[1:2] + fcz * column[2:3] + fsz * column[3:4]
    energy_ref[...] = (0.01 / total) * energy
    force_scale = 0.04 * math.pi / math.sqrt(total)
    potential_scale = 0.4 / math.sqrt(total)

    for s in range(steps2):
        lanes = pl.ds(s * tile2, tile2)
        values = force_a(1, lanes) + force_b(1, lanes)
        phi, grad_x, grad_z, grad_y, grad_zb = (v + acc_ref[k : k + 1, lanes] for k, v in enumerate(values))
        charge = ions_ref[3:4, lanes]
        fcosy, fsiny, fcosz, fsinz = (far_ref[k : k + 1, lanes] for k in range(4))
        phi += fcy * fcosy + fsy * fsiny + fcz * fcosz + fsz * fsinz
        far_y = 32.0 * (fsy * fcosy - fcy * fsiny)
        far_z = 32.0 * (fsz * fcosz - fcz * fsinz)
        out_ref[0:1, lanes] = -force_scale * (charge * grad_x)
        out_ref[1:2, lanes] = -force_scale * (grad_y + charge * far_y)
        out_ref[2:3, lanes] = -force_scale * (grad_zb + charge * (grad_z + far_z))
        out_ref[3:4, lanes] = potential_scale * phi

    for h, (first, second) in enumerate(((swap0, forward0), (swap1, forward1))):
        first.wait_send()
        all_bytes(h, 2)
        all_bytes(h, 4)
        second.wait_send()


def per_device(ions, col_ids):
    count = ions.shape[1]
    total = count * lax.axis_size("kcol") * lax.axis_size("ion")
    forces, energy = pl.pallas_call(
        functools.partial(kernel, 512, 256, total),
        out_shape=(jax.ShapeDtypeStruct(ions.shape, F32), jax.ShapeDtypeStruct((1, 1), F32)),
        in_specs=[pl.BlockSpec(memory_space=pltpu.VMEM)] * 2,
        out_specs=[pl.BlockSpec(memory_space=pltpu.VMEM)] * 2,
        scratch_shapes=[
            pltpu.VMEM((64, count), F32),
            pltpu.VMEM((64, count), F32),
            pltpu.VMEM((16, count), F32),
            pltpu.VMEM((8, count), F32),
            pltpu.VMEM((8, count), F32),
            pltpu.VMEM((NA, count), BF16),
            pltpu.VMEM((NA, count), BF16),
            pltpu.VMEM((NB, count), BF16),
            pltpu.VMEM((NB, count), BF16),
            pltpu.VMEM((NA, NB), F32),
            pltpu.VMEM((2, 128, NB), F32),
            pltpu.VMEM((2, 128, NB), F32),
            pltpu.VMEM((2, 63, 8, 128), F32),
            pltpu.VMEM((2, 8, 128), F32),
            pltpu.VMEM((NA, NB), F32),
            pltpu.VMEM((NA, NB), F32),
            pltpu.VMEM((NA, NB), BF16),
            pltpu.VMEM((NA, NB), BF16),
            pltpu.VMEM((NB, NA), BF16),
            pltpu.VMEM((NB, NA), BF16),
            pltpu.SemaphoreType.DMA((2, 8)),
        ],
        compiler_params=pltpu.CompilerParams(
            collective_id=0, has_side_effects=True, vmem_limit_bytes=VMEM_LIMIT
        ),
    )(ions, col_ids.reshape(1, -1))
    return forces, energy.reshape(())


def solution(mesh):
    return jax.shard_map(
        per_device,
        mesh=mesh,
        in_specs=(P(None, ("kcol", "ion")), P("kcol")),
        out_specs=(P(None, ("kcol", "ion")), P()),
        check_vma=False,
    )
```

```python
import functools
import math

import jax
import jax.numpy as jnp
from jax import lax
from jax.experimental import pallas as pl
from jax.experimental.pallas import tpu as pltpu
from jax.sharding import PartitionSpec as P

NA = 512
NB = 512
VMEM_LIMIT = 60 * 1024 * 1024
CUT = 3
LATE = 3
F32 = jnp.float32
BF16 = jnp.bfloat16
F8 = jnp.float8_e4m3fn
LOW = 1024.0
COS = [(-1.0) ** k / math.factorial(2 * k) for k in range(8)]
SIN = [(-1.0) ** k / math.factorial(2 * k + 1) for k in range(7)]


def cos_sin(turns):
    half = jnp.floor(2.0 * turns + 0.5)
    rest = turns - 0.5 * half
    sign = 1.0 - 4.0 * (0.5 * half - jnp.floor(0.5 * half))
    angle = (2.0 * math.pi) * rest
    square = angle * angle
    cosine = jnp.full_like(square, COS[-1])
    for c in COS[-2::-1]:
        cosine = cosine * square + c
    sine = jnp.full_like(square, SIN[-1])
    for c in SIN[-2::-1]:
        sine = sine * square + c
    return cosine * sign, sine * angle * sign


def rows(count, width):
    return lax.broadcasted_iota(jnp.int32, (count, width), 0).astype(F32)


def base_tables(block):
    width = block.shape[1]
    wave = rows(32, width)
    cx, sx = cos_sin(wave * block[0:1])
    cy, sy = cos_sin(wave * block[1:2])
    eight = rows(8, width)
    freq = jnp.where(eight < 4.0, eight + 0.5, 8.0 * eight - 28.5)
    cz, sz = cos_sin(freq * block[2:3])
    return wave, cx, sx, cy, sy, freq, cz, sz


def split(value):
    high = value.astype(BF16)
    low = (value - high.astype(F32)).astype(BF16)
    return high, low


def build(block, base, a_hi, a_lo, b_hi, b_lo, lanes):
    wave, cx, sx, cy, sy, freq, cz, sz = base
    tx = jnp.concatenate([cx, sx], 0)
    charge = block[3:4]
    for r in range(4):
        for cs, table in enumerate((cz, sz)):
            at = pl.ds(r * 128 + cs * 64, 64)
            high, low = split((charge * table[r : r + 1]) * tx)
            a_hi[at, lanes] = high
            a_lo[at, lanes] = low
    for cs, table in enumerate((cz, sz)):
        for ycs, ty in enumerate((cy, sy)):
            for p in range(4):
                at = pl.ds(cs * 256 + ycs * 128 + p * 32, 32)
                high, low = split(table[4 + p : 5 + p] * ty)
                b_hi[at, lanes] = high
                b_lo[at, lanes] = low


def dot_nt(a, b):
    return lax.dot_general(a, b, (((1,), (1,)), ((), ())), preferred_element_type=F32)


def mask_rows(ids):
    my = lax.shift_right_logical(ids, 6) - 32
    mz = (ids & 63) - 32
    ay, az = jnp.abs(my), jnp.abs(mz)
    low = az & 7
    plus = low >= 4
    r = jnp.where(plus, low - 4, 3 - low)
    row = r * 8 + jnp.where(plus, 0, 4) + jnp.where(my < 0, 2, 0) + jnp.where(mz < 0, 1, 0)
    lane = lax.shift_right_logical(az, 3) * 32 + ay
    row = jnp.where((ay > 31) | (az > 31), -1, row)
    count = ids.shape[1]
    left = (lax.broadcasted_iota(jnp.int32, (32, count), 0) == row).astype(F32).astype(BF16)
    right = (lax.broadcasted_iota(jnp.int32, (128, count), 0) == lane).astype(F32).astype(BF16)
    return dot_nt(left, right)


def weights(h, t_ref, d_ref):
    lane = lax.broadcasted_iota(jnp.int32, (16, 128), 1)
    my = (lane & 31).astype(F32)
    p = lax.shift_right_logical(lane, 5).astype(F32)
    energy = jnp.zeros((16, 128), F32)
    largest = jnp.zeros((16, 128), F32)
    copies = 1.0 / lax.axis_size("ion")
    for r in (2 * h, 2 * h + 1):
        masks = [
            t_ref[r * 128 + k // 4 * 64 + 32 : r * 128 + k // 4 * 64 + 33, k % 4 * 128 : k % 4 * 128 + 128] * copies
            for k in range(8)
        ]
        for half in range(2):
            mx = rows(16, 128) + 16.0 * half
            tt = {}
            for zr in range(2):
                for x in range(2):
                    for zp in range(2):
                        for y in range(2):
                            tt[zr, x, zp, y] = t_ref[
                                pl.ds(r * 128 + zr * 64 + x * 32 + half * 16, 16),
                                pl.ds(zp * 256 + y * 128, 128),
                            ]
                            if x == 1 and half == 0:
                                tt[zr, x, zp, y] = jnp.where(mx == 0.0, 0.0, tt[zr, x, zp, y])
                            if (r, half, zr, x, zp, y) == (0, 0, 0, 0, 0, 1):
                                tt[zr, x, zp, y] = jnp.where(my == 0.0, 0.0, tt[zr, x, zp, y])
            dd = {}
            parts = {}
            for sgn in range(2):
                mz = 8.0 * p + (4.0 + r if sgn == 0 else 3.0 - r)
                m2 = mx * mx + my * my + mz * mz
                live = (m2 <= 1024.0) & (m2 > 0.0)
                h = jnp.where(mx == 0.0, 0.5, 1.0)
                w = jnp.where(live, h * jnp.exp(m2 * (-1.0 / 1600.0)) / jnp.maximum(m2, 1.0), 0.0)
                at = sgn * 4
                mpp, mpm, mmp, mmm = masks[at : at + 4]
                ws1, wd1 = w * (mpp + mmm), w * (mpp - mmm)
                ws2, wd2 = w * (mpm + mmp), w * (mpm - mmp)
                s = 1.0 if sgn == 0 else -1.0
                z = {}
                for x in range(2):
                    for y in range(2):
                        z[x, y, 0] = tt[0, x, 0, y] - s * tt[1, x, 1, y]
                        z[x, y, 1] = tt[0, x, 1, y] + s * tt[1, x, 0, y]
                um = [z[x, 0, 0] - z[x, 1, 1] for x in range(2)]
                up = [z[x, 0, 0] + z[x, 1, 1] for x in range(2)]
                vp = [z[x, 1, 0] + z[x, 0, 1] for x in range(2)]
                vm = [z[x, 1, 0] - z[x, 0, 1] for x in range(2)]
                um2 = [ws1 * um[0] - wd1 * vp[1], ws1 * um[1] + wd1 * vp[0]]
                vp2 = [ws1 * vp[0] + wd1 * um[1], ws1 * vp[1] - wd1 * um[0]]
                up2 = [ws2 * up[0] - wd2 * vm[1], ws2 * up[1] + wd2 * vm[0]]
                vm2 = [ws2 * vm[0] + wd2 * up[1], ws2 * vm[1] - wd2 * up[0]]
                for x in range(2):
                    energy += um[x] * um2[x] + vp[x] * vp2[x] + up[x] * up2[x] + vm[x] * vm2[x]
                    parts[sgn, x, 0, 0] = um2[x] + up2[x]
                    parts[sgn, x, 1, 1] = up2[x] - um2[x]
                    parts[sgn, x, 1, 0] = vp2[x] + vm2[x]
                    parts[sgn, x, 0, 1] = vp2[x] - vm2[x]
            for x in range(2):
                for y in range(2):
                    dd[0, x, 0, y] = parts[0, x, y, 0] + parts[1, x, y, 0]
                    dd[1, x, 1, y] = parts[1, x, y, 0] - parts[0, x, y, 0]
                    dd[0, x, 1, y] = parts[0, x, y, 1] + parts[1, x, y, 1]
                    dd[1, x, 0, y] = parts[0, x, y, 1] - parts[1, x, y, 1]
            for (zr, x, zp, y), value in dd.items():
                at = (pl.ds(r * 128 + zr * 64 + x * 32 + half * 16, 16), pl.ds(zp * 256 + y * 128, 128))
                d_ref[at] = value
                largest = jnp.maximum(largest, jnp.abs(value))
    return energy, largest


MESH = pl.DeviceIdType.MESH


def hops(step):
    return sum(min(d, 4 - d) for d in (step >> 4, (step >> 2) & 3, step & 3))


ORDER = sorted(range(1, 64), key=lambda step: -hops(step))


def place():
    k, i = lax.axis_index("kcol"), lax.axis_index("ion")
    return i >> 1, k >> 2, (k & 2) | (i & 1), k & 1


def device(x, y, z, core):
    return {"kcol": (y << 2) | (z & 2) | core, "ion": (x << 1) | (z & 1)}


def peer(me, step):
    x, y, z, core = me
    return (x + (step >> 4)) & 3, (y + ((step >> 2) & 3)) & 3, (z + (step & 3)) & 3, core


def chip(where):
    return where[0] * 16 + where[1] * 4 + where[2]


def tile_of(index, row0):
    row = pl.multiple_of(row0 + (index >> 2) * 8, 8)
    return pl.ds(row, 8), pl.ds(pl.multiple_of((index & 3) * 128, 128), 128)


def kernel(
    tile,
    tile2,
    total,
    ions_ref,
    ids_ref,
    out_ref,
    energy_ref,
    tx_ref,
    ty_ref,
    tz_ref,
    far_ref,
    acc_ref,
    a_hi,
    a_lo,
    b_hi,
    b_lo,
    t_loc,
    sib,
    own,
    parts,
    red,
    full,
    d_ref,
    d_hi,
    dt_hi,
    a_8,
    b_8,
    d_8,
    dt_8,
    sems,
):
    ions = ions_ref.shape[1]
    me = place()
    core = me[3]
    sibling = device(me[0], me[1], me[2], 1 - core)
    barrier = pltpu.get_barrier_semaphore()

    for step in ORDER:
        pl.semaphore_signal(barrier, inc=1, device_id=device(*peer(me, step)), device_id_type=MESH)
    pl.semaphore_signal(barrier, inc=1, device_id=sibling, device_id_type=MESH)

    def to_sibling(h, k, src, dst):
        return pltpu.make_async_remote_copy(
            src_ref=src,
            dst_ref=dst,
            send_sem=sems.at[h, k],
            recv_sem=sems.at[h, k + 1],
            device_id=sibling,
            device_id_type=MESH,
        )

    def all_bytes(h, k):
        pltpu.make_async_copy(parts.at[h], parts.at[h], sems.at[h, k]).wait()

    wave = rows(32, tile)
    freq = rows(8, tile)
    freq = jnp.where(freq < 4.0, freq + 0.5, 8.0 * freq - 28.5)

    def t_block(h, first, last):
        for s in range(first, last):
            lanes = pl.ds(s * tile, tile)
            at = pl.ds(h * 256, 256)
            high = a_hi[at, lanes]
            left = jnp.concatenate([high, high, a_lo[at, lanes]], 1)
            right = jnp.concatenate([b_hi[:, lanes], b_lo[:, lanes], b_hi[:, lanes]], 1)
            product = dot_nt(left, right)
            if s == 0:
                t_loc[at] = product
            else:
                t_loc[at] += product

    far = jnp.zeros((8, 128), F32)
    for s in range(ions // tile):
        lanes = pl.ds(s * tile, tile)
        block = ions_ref[:, lanes]
        base = base_tables(block)
        _, cx, sx, cy, sy, _, cz, sz = base
        tx_ref[0:32, lanes] = cx
        tx_ref[32:64, lanes] = sx
        ty_ref[0:32, lanes] = cy
        ty_ref[32:64, lanes] = sy
        tz_ref[0:8, lanes] = cz
        tz_ref[8:16, lanes] = sz
        build(block, base, a_hi, a_lo, b_hi, b_lo, lanes)
        turns = 32.0 * block[1:3]
        fc, fs = cos_sin(turns)
        four = jnp.concatenate([fc[0:1], fs[0:1], fc[1:2], fs[1:2]], 0)
        far_ref[0:4, lanes] = four
        value = jnp.concatenate([block[3:4] * four, jnp.zeros((4, tile), F32)], 0)
        for c in range(tile // 128):
            far += value[:, c * 128 : (c + 1) * 128]
        t_block(0, s, s + 1)

    ids = ids_ref[...]
    masks = mask_rows(ids)

    def patch(h):
        for k in range(16 * h, 16 * h + 16):
            t_loc[64 * (k // 4) + 32 : 64 * (k // 4) + 33, k % 4 * 128 : k % 4 * 128 + 128] = masks[k : k + 1]
        if h == 0:
            row = lax.broadcasted_iota(jnp.int32, (8, 128), 0)
            flags = far
            flags = jnp.where(row == 4, (ids == 32).astype(F32), flags)
            flags = jnp.where(row == 5, (ids == 2048).astype(F32), flags)
            lane = lax.broadcasted_iota(jnp.int32, (8, 128), 1)
            column = jnp.sum(flags, 1, keepdims=True)
            t_loc[0:8, 128:256] = jnp.where(lane == 0, column, t_loc[0:8, 128:256])

    def swap(h):
        theirs = pl.ds(pl.multiple_of(256 * h + 128 * (1 - core), 128), 128)
        return to_sibling(h, 0, t_loc.at[theirs], sib.at[h])

    def scatter(h):
        mine = pl.ds(pl.multiple_of(256 * h + 128 * core, 128), 128)
        own[h] = t_loc[mine] + sib[h]

        for step in ORDER:
            other = peer(me, step)
            r, l = tile_of(chip(other), 0)
            pltpu.make_async_remote_copy(
                src_ref=own.at[h, r, l],
                dst_ref=parts.at[h, step - 1],
                send_sem=sems.at[h, 2],
                recv_sem=sems.at[h, 3],
                device_id=device(*other),
                device_id_type=MESH,
            ).start()

    def gather(h):
        all_bytes(h, 3)
        r, l = tile_of(chip(me), 0)
        red[h] = own[h, r, l] + jnp.sum(parts[h], 0)
        where = tile_of(chip(me), 256 * h + 128 * core)
        full[where] = red[h]

        for step in ORDER:
            pltpu.make_async_remote_copy(
                src_ref=red.at[h],
                dst_ref=full.at[where],
                send_sem=sems.at[h, 4],
                recv_sem=sems.at[h, 5],
                device_id=device(*peer(me, step)),
                device_id_type=MESH,
            ).start()

    def forward(h):
        mine = full.at[pl.ds(pl.multiple_of(256 * h + 128 * core, 128), 128)]
        return to_sibling(h, 6, mine, mine)

    def small_tables():
        for s in range(ions // tile):
            lanes = pl.ds(s * tile, tile)
            for high, low, to in ((a_hi, a_lo, a_8), (b_hi, b_lo, b_8)):
                for k in range(0, NA, 64):
                    at = pl.ds(k, 64)
                    to[0, at, lanes] = (low[at, lanes].astype(F32) * LOW).astype(F8)
                    to[1, at, lanes] = high[at, lanes].astype(F32).astype(F8)

    def small(block, low, scale):
        return (block * scale).astype(F8), (low.astype(F32) * (scale * LOW)).astype(F8)

    def transpose(h, largest):
        largest = jnp.max(jnp.max(largest, 1, keepdims=True), 0, keepdims=True)
        scale = 128.0 / jnp.maximum(largest, 1e-30)
        for i in (2 * h, 2 * h + 1):
            for j in range(NB // 128):
                block = d_ref[i * 128 : (i + 1) * 128, j * 128 : (j + 1) * 128]
                at = (pl.ds(i * 128, 128), pl.ds(j * 128, 128))
                high, low = split(block)
                d_hi[at] = high
                d_8[0, *at], d_8[1, *at] = small(block, low, scale)
                block = block.T
                at = (pl.ds(j * 128, 128), pl.ds(i * 128, 128))
                high, low = split(block)
                dt_hi[at] = high
                dt_8[0, *at], dt_8[1, *at] = small(block, low, scale)
        return 1.0 / (scale * LOW)

    def z_rows(lanes, k):
        cz, sz = tz_ref[k : k + 1, lanes], tz_ref[8 + k : 9 + k, lanes]
        f = k + 0.5 if k < 4 else 8.0 * k - 28.5
        return (cz, sz), (-f * sz, f * cz)

    def force_a(h, lanes, back):
        at = pl.ds(h * 256, 256)
        h_a = jnp.dot(d_hi[at], b_hi[:, lanes], preferred_element_type=F32)
        cross = jnp.dot(
            jnp.concatenate([d_8[0, at], d_8[1, at]], 1),
            jnp.concatenate([b_8[0, :, lanes], b_8[1, :, lanes]], 0),
            preferred_element_type=F32,
        )
        h_a += back * cross
        v0 = vz = None
        for k in range(2):
            z, dz = z_rows(lanes, 2 * h + k)
            for cs in range(2):
                part = h_a[k * 128 + cs * 64 : k * 128 + cs * 64 + 64]
                v0 = z[cs] * part if v0 is None else v0 + z[cs] * part
                vz = dz[cs] * part if vz is None else vz + dz[cs] * part
        cx, sx = tx_ref[0:32, lanes], tx_ref[32:64, lanes]
        n = rows(32, tile2)
        phi = jnp.sum(cx * v0[:32] + sx * v0[32:], 0, keepdims=True)
        grad_x = jnp.sum(n * (cx * v0[32:] - sx * v0[:32]), 0, keepdims=True)
        grad_z = jnp.sum(cx * vz[:32] + sx * vz[32:], 0, keepdims=True)
        return phi, grad_x, grad_z

    def force_b(h, lanes, back):
        at = pl.ds(h * 256, 256)
        h_b = jnp.dot(dt_hi[:, at], a_hi[at, lanes], preferred_element_type=F32)
        cross = jnp.dot(
            jnp.concatenate([dt_8[0, :, at], dt_8[1, :, at]], 1),
            jnp.concatenate([a_8[0, at, lanes], a_8[1, at, lanes]], 0),
            preferred_element_type=F32,
        )
        h_b += back * cross
        u0, uz = [None, None], [None, None]
        for p in range(4):
            z, dz = z_rows(lanes, 4 + p)
            for cs in range(2):
                for ycs in range(2):
                    at = cs * 256 + ycs * 128 + p * 32
                    part = h_b[at : at + 32]
                    u0[ycs] = z[cs] * part if u0[ycs] is None else u0[ycs] + z[cs] * part
                    uz[ycs] = dz[cs] * part if uz[ycs] is None else uz[ycs] + dz[cs] * part
        cy, sy = ty_ref[0:32, lanes], ty_ref[32:64, lanes]
        n = rows(32, tile2)
        grad_y = jnp.sum(n * (cy * u0[1] - sy * u0[0]), 0, keepdims=True)
        grad_z = jnp.sum(cy * uz[0] + sy * uz[1], 0, keepdims=True)
        return grad_y, grad_z

    steps = ions // tile
    patch(0)
    pl.semaphore_wait(barrier, 64)
    swap0 = swap(0)
    swap0.start()
    t_block(1, 0, CUT)
    swap0.wait_recv()
    scatter(0)
    t_block(1, CUT, steps)
    patch(1)
    swap1 = swap(1)
    swap1.start()
    swap1.wait_recv()
    scatter(1)
    small_tables()
    gather(0)
    gather(1)
    all_bytes(0, 5)
    forward0 = forward(0)
    forward0.start()
    forward0.wait_recv()
    energy, largest = weights(0, full, d_ref)
    back = transpose(0, largest)
    forward1 = forward(1)
    steps2 = ions // tile2
    for s in range(steps2):
        lanes = pl.ds(s * tile2, tile2)
        if s == steps2 - LATE:
            all_bytes(1, 5)
            forward1.start()
        for k, value in enumerate(force_a(0, lanes, back) + force_b(0, lanes, back)):
            acc_ref[k : k + 1, lanes] = value
    forward1.wait_recv()
    more, largest = weights(1, full, d_ref)
    energy += more
    back = transpose(1, largest)

    copies = 1.0 / lax.axis_size("ion")
    column = full[0:8, 128:129]
    far_weight = 0.5 * math.exp(-1024.0 / 1600.0) / 1024.0
    wy = far_weight * copies * column[4:5]
    wz = far_weight * copies * column[5:6]
    fcy, fsy, fcz, fsz = wy * column[0:1], wy * column[1:2], wz * column[2:3], wz * column[3:4]
    energy = jnp.sum(jnp.sum(energy, 1, keepdims=True), 0, keepdims=True)
    energy += fcy * column[0:1] + fsy * column[1:2] + fcz * column[2:3] + fsz * column[3:4]
    energy_ref[...] = (0.01 / total) * energy
    force_scale = 0.04 * math.pi / math.sqrt(total)
    potential_scale = 0.4 / math.sqrt(total)

    for s in range(steps2):
        lanes = pl.ds(s * tile2, tile2)
        values = force_a(1, lanes, back) + force_b(1, lanes, back)
        phi, grad_x, grad_z, grad_y, grad_zb = (v + acc_ref[k : k + 1, lanes] for k, v in enumerate(values))
        charge = ions_ref[3:4, lanes]
        fcosy, fsiny, fcosz, fsinz = (far_ref[k : k + 1, lanes] for k in range(4))
        phi += fcy * fcosy + fsy * fsiny + fcz * fcosz + fsz * fsinz
        far_y = 32.0 * (fsy * fcosy - fcy * fsiny)
        far_z = 32.0 * (fsz * fcosz - fcz * fsinz)
        out_ref[0:1, lanes] = -force_scale * (charge * grad_x)
        out_ref[1:2, lanes] = -force_scale * (grad_y + charge * far_y)
        out_ref[2:3, lanes] = -force_scale * (grad_zb + charge * (grad_z + far_z))
        out_ref[3:4, lanes] = potential_scale * phi

    for h, (first, second) in enumerate(((swap0, forward0), (swap1, forward1))):
        first.wait_send()
        all_bytes(h, 2)
        all_bytes(h, 4)
        second.wait_send()


def per_device(ions, col_ids):
    count = ions.shape[1]
    total = count * lax.axis_size("kcol") * lax.axis_size("ion")
    forces, energy = pl.pallas_call(
        functools.partial(kernel, 512, 256, total),
        out_shape=(jax.ShapeDtypeStruct(ions.shape, F32), jax.ShapeDtypeStruct((1, 1), F32)),
        in_specs=[pl.BlockSpec(memory_space=pltpu.VMEM)] * 2,
        out_specs=[pl.BlockSpec(memory_space=pltpu.VMEM)] * 2,
        scratch_shapes=[
            pltpu.VMEM((64, count), F32),
            pltpu.VMEM((64, count), F32),
            pltpu.VMEM((16, count), F32),
            pltpu.VMEM((8, count), F32),
            pltpu.VMEM((8, count), F32),
            pltpu.VMEM((NA, count), BF16),
            pltpu.VMEM((NA, count), BF16),
            pltpu.VMEM((NB, count), BF16),
            pltpu.VMEM((NB, count), BF16),
            pltpu.VMEM((NA, NB), F32),
            pltpu.VMEM((2, 128, NB), F32),
            pltpu.VMEM((2, 128, NB), F32),
            pltpu.VMEM((2, 63, 8, 128), F32),
            pltpu.VMEM((2, 8, 128), F32),
            pltpu.VMEM((NA, NB), F32),
            pltpu.VMEM((NA, NB), F32),
            pltpu.VMEM((NA, NB), BF16),
            pltpu.VMEM((NB, NA), BF16),
            pltpu.VMEM((2, NA, count), F8),
            pltpu.VMEM((2, NB, count), F8),
            pltpu.VMEM((2, NA, NB), F8),
            pltpu.VMEM((2, NB, NA), F8),
            pltpu.SemaphoreType.DMA((2, 8)),
        ],
        compiler_params=pltpu.CompilerParams(
            collective_id=0, has_side_effects=True, vmem_limit_bytes=VMEM_LIMIT
        ),
    )(ions, col_ids.reshape(1, -1))
    return forces, energy.reshape(())


def solution(mesh):
    return jax.shard_map(
        per_device,
        mesh=mesh,
        in_specs=(P(None, ("kcol", "ion")), P("kcol")),
        out_specs=(P(None, ("kcol", "ion")), P()),
        check_vma=False,
    )
```

```python
import functools
import math

import jax
import jax.numpy as jnp
from jax import lax
from jax.experimental import pallas as pl
from jax.experimental.pallas import tpu as pltpu
from jax.sharding import PartitionSpec as P

NA = 512
NB = 512
VMEM_LIMIT = 60 * 1024 * 1024
CUT = 3
LATE = 5
F32 = jnp.float32
BF16 = jnp.bfloat16
F8 = jnp.float8_e4m3fn
LOW = 1024.0
A_UNIT = 32.0
B_UNIT = 48.0
COS = [(-1.0) ** k / math.factorial(2 * k) for k in range(8)]
SIN = [(-1.0) ** k / math.factorial(2 * k + 1) for k in range(7)]


def cos_sin(turns):
    half = jnp.floor(2.0 * turns + 0.5)
    rest = turns - 0.5 * half
    sign = 1.0 - 4.0 * (0.5 * half - jnp.floor(0.5 * half))
    angle = (2.0 * math.pi) * rest
    square = angle * angle
    cosine = jnp.full_like(square, COS[-1])
    for c in COS[-2::-1]:
        cosine = cosine * square + c
    sine = jnp.full_like(square, SIN[-1])
    for c in SIN[-2::-1]:
        sine = sine * square + c
    return cosine * sign, sine * angle * sign


def rows(count, width):
    return lax.broadcasted_iota(jnp.int32, (count, width), 0).astype(F32)


def base_tables(block):
    width = block.shape[1]
    wave = rows(32, width)
    cx, sx = cos_sin(wave * block[0:1])
    cy, sy = cos_sin(wave * block[1:2])
    eight = rows(8, width)
    freq = jnp.where(eight < 4.0, eight + 0.5, 8.0 * eight - 28.5)
    cz, sz = cos_sin(freq * block[2:3])
    return wave, cx, sx, cy, sy, freq, cz, sz


def split(value):
    high = value.astype(BF16)
    low = (value - high.astype(F32)).astype(BF16)
    return high, low


def build_a(h, charge, tx, cz, sz, a_hi, a_lo, lanes):
    for r in (2 * h, 2 * h + 1):
        for cs, table in enumerate((cz, sz)):
            at = pl.ds(r * 128 + cs * 64, 64)
            high, low = split((charge * table[r : r + 1]) * tx)
            a_hi[at, lanes] = high
            a_lo[at, lanes] = low


def build_b(cy, sy, cz, sz, b_hi, b_lo, lanes):
    for cs, table in enumerate((cz, sz)):
        for ycs, ty in enumerate((cy, sy)):
            for p in range(4):
                at = pl.ds(cs * 256 + ycs * 128 + p * 32, 32)
                high, low = split(table[4 + p : 5 + p] * ty)
                b_hi[at, lanes] = high
                b_lo[at, lanes] = low


def dot_nt(a, b):
    return lax.dot_general(a, b, (((1,), (1,)), ((), ())), preferred_element_type=F32)


def mask_rows(ids):
    my = lax.shift_right_logical(ids, 6) - 32
    mz = (ids & 63) - 32
    ay, az = jnp.abs(my), jnp.abs(mz)
    low = az & 7
    plus = low >= 4
    r = jnp.where(plus, low - 4, 3 - low)
    row = r * 8 + jnp.where(plus, 0, 4) + jnp.where(my < 0, 2, 0) + jnp.where(mz < 0, 1, 0)
    lane = lax.shift_right_logical(az, 3) * 32 + ay
    row = jnp.where((ay > 31) | (az > 31), -1, row)
    count = ids.shape[1]
    left = (lax.broadcasted_iota(jnp.int32, (32, count), 0) == row).astype(F32).astype(BF16)
    right = (lax.broadcasted_iota(jnp.int32, (128, count), 0) == lane).astype(F32).astype(BF16)
    return dot_nt(left, right)


def spread_a(mx):
    return jnp.sqrt(mx * mx + 1.0)


def spread_b(my, p):
    mz = 8.0 * p + 3.5
    return jnp.sqrt(my * my + mz * mz)


def lane_waves():
    lane = lax.broadcasted_iota(jnp.int32, (128, 128), 1)
    return (lane & 31).astype(F32), lax.shift_right_logical(lane, 5).astype(F32)


def row_waves():
    row = lax.broadcasted_iota(jnp.int32, (128, 128), 0)
    return (row & 31).astype(F32), lax.shift_right_logical(row, 5).astype(F32)


def weights(h, t_ref, d_ref):
    lane = lax.broadcasted_iota(jnp.int32, (16, 128), 1)
    my = (lane & 31).astype(F32)
    p = lax.shift_right_logical(lane, 5).astype(F32)
    energy = jnp.zeros((16, 128), F32)
    largest = jnp.zeros((16, 128), F32)
    copies = 1.0 / lax.axis_size("ion")
    for r in (2 * h, 2 * h + 1):
        masks = [
            t_ref[r * 128 + k // 4 * 64 + 32 : r * 128 + k // 4 * 64 + 33, k % 4 * 128 : k % 4 * 128 + 128] * copies
            for k in range(8)
        ]
        for half in range(2):
            mx = rows(16, 128) + 16.0 * half
            even = spread_a(mx) * spread_b(my, p)
            tt = {}
            for zr in range(2):
                for x in range(2):
                    for zp in range(2):
                        for y in range(2):
                            tt[zr, x, zp, y] = t_ref[
                                pl.ds(r * 128 + zr * 64 + x * 32 + half * 16, 16),
                                pl.ds(zp * 256 + y * 128, 128),
                            ]
                            if x == 1 and half == 0:
                                tt[zr, x, zp, y] = jnp.where(mx == 0.0, 0.0, tt[zr, x, zp, y])
                            if (r, half, zr, x, zp, y) == (0, 0, 0, 0, 0, 1):
                                tt[zr, x, zp, y] = jnp.where(my == 0.0, 0.0, tt[zr, x, zp, y])
            dd = {}
            parts = {}
            for sgn in range(2):
                mz = 8.0 * p + (4.0 + r if sgn == 0 else 3.0 - r)
                m2 = mx * mx + my * my + mz * mz
                live = (m2 <= 1024.0) & (m2 > 0.0)
                h = jnp.where(mx == 0.0, 0.5, 1.0)
                w = jnp.where(live, h * jnp.exp(m2 * (-1.0 / 1600.0)) / jnp.maximum(m2, 1.0), 0.0)
                at = sgn * 4
                mpp, mpm, mmp, mmm = masks[at : at + 4]
                ws1, wd1 = w * (mpp + mmm), w * (mpp - mmm)
                ws2, wd2 = w * (mpm + mmp), w * (mpm - mmp)
                s = 1.0 if sgn == 0 else -1.0
                z = {}
                for x in range(2):
                    for y in range(2):
                        z[x, y, 0] = tt[0, x, 0, y] - s * tt[1, x, 1, y]
                        z[x, y, 1] = tt[0, x, 1, y] + s * tt[1, x, 0, y]
                um = [z[x, 0, 0] - z[x, 1, 1] for x in range(2)]
                up = [z[x, 0, 0] + z[x, 1, 1] for x in range(2)]
                vp = [z[x, 1, 0] + z[x, 0, 1] for x in range(2)]
                vm = [z[x, 1, 0] - z[x, 0, 1] for x in range(2)]
                um2 = [ws1 * um[0] - wd1 * vp[1], ws1 * um[1] + wd1 * vp[0]]
                vp2 = [ws1 * vp[0] + wd1 * um[1], ws1 * vp[1] - wd1 * um[0]]
                up2 = [ws2 * up[0] - wd2 * vm[1], ws2 * up[1] + wd2 * vm[0]]
                vm2 = [ws2 * vm[0] + wd2 * up[1], ws2 * vm[1] - wd2 * up[0]]
                for x in range(2):
                    energy += um[x] * um2[x] + vp[x] * vp2[x] + up[x] * up2[x] + vm[x] * vm2[x]
                    parts[sgn, x, 0, 0] = um2[x] + up2[x]
                    parts[sgn, x, 1, 1] = up2[x] - um2[x]
                    parts[sgn, x, 1, 0] = vp2[x] + vm2[x]
                    parts[sgn, x, 0, 1] = vp2[x] - vm2[x]
            for x in range(2):
                for y in range(2):
                    dd[0, x, 0, y] = parts[0, x, y, 0] + parts[1, x, y, 0]
                    dd[1, x, 1, y] = parts[1, x, y, 0] - parts[0, x, y, 0]
                    dd[0, x, 1, y] = parts[0, x, y, 1] + parts[1, x, y, 1]
                    dd[1, x, 0, y] = parts[0, x, y, 1] - parts[1, x, y, 1]
            for (zr, x, zp, y), value in dd.items():
                at = (pl.ds(r * 128 + zr * 64 + x * 32 + half * 16, 16), pl.ds(zp * 256 + y * 128, 128))
                d_ref[at] = value
                largest = jnp.maximum(largest, jnp.abs(value) * even)
    return energy, largest


MESH = pl.DeviceIdType.MESH


def hops(step):
    return sum(min(d, 4 - d) for d in (step >> 4, (step >> 2) & 3, step & 3))


ORDER = sorted(range(1, 64), key=lambda step: -hops(step))


def place():
    k, i = lax.axis_index("kcol"), lax.axis_index("ion")
    return i >> 1, k >> 2, (k & 2) | (i & 1), k & 1


def device(x, y, z, core):
    return {"kcol": (y << 2) | (z & 2) | core, "ion": (x << 1) | (z & 1)}


def peer(me, step):
    x, y, z, core = me
    return (x + (step >> 4)) & 3, (y + ((step >> 2) & 3)) & 3, (z + (step & 3)) & 3, core


def chip(where):
    return where[0] * 16 + where[1] * 4 + where[2]


def tile_of(index, row0):
    row = pl.multiple_of(row0 + (index >> 2) * 8, 8)
    return pl.ds(row, 8), pl.ds(pl.multiple_of((index & 3) * 128, 128), 128)


def kernel(
    tile,
    tile2,
    total,
    ions_ref,
    ids_ref,
    out_ref,
    energy_ref,
    tx_ref,
    ty_ref,
    tz_ref,
    far_ref,
    acc_ref,
    a_hi,
    a_lo,
    b_hi,
    b_lo,
    t_loc,
    sib,
    own,
    parts,
    red,
    full,
    d_ref,
    d_hi,
    dt_hi,
    a_8,
    b_8,
    d_8,
    dt_8,
    inv,
    sems,
):
    ions = ions_ref.shape[1]
    me = place()
    core = me[3]
    sibling = device(me[0], me[1], me[2], 1 - core)
    barrier = pltpu.get_barrier_semaphore()

    for step in ORDER:
        pl.semaphore_signal(barrier, inc=1, device_id=device(*peer(me, step)), device_id_type=MESH)
    pl.semaphore_signal(barrier, inc=1, device_id=sibling, device_id_type=MESH)

    def to_sibling(h, k, src, dst):
        return pltpu.make_async_remote_copy(
            src_ref=src,
            dst_ref=dst,
            send_sem=sems.at[h, k],
            recv_sem=sems.at[h, k + 1],
            device_id=sibling,
            device_id_type=MESH,
        )

    def all_bytes(h, k):
        pltpu.make_async_copy(parts.at[h], parts.at[h], sems.at[h, k]).wait()

    wave = rows(32, tile)
    freq = rows(8, tile)
    freq = jnp.where(freq < 4.0, freq + 0.5, 8.0 * freq - 28.5)

    def t_block(h, first, last):
        for s in range(first, last):
            lanes = pl.ds(s * tile, tile)
            if h == 1:
                build_a(1, ions_ref[3:4, lanes], tx_ref[:, lanes], tz_ref[0:8, lanes], tz_ref[8:16, lanes], a_hi, a_lo, lanes)
            at = pl.ds(h * 256, 256)
            high = a_hi[at, lanes]
            left = jnp.concatenate([high, high, a_lo[at, lanes]], 1)
            right = jnp.concatenate([b_hi[:, lanes], b_lo[:, lanes], b_hi[:, lanes]], 1)
            product = dot_nt(left, right)
            if s == 0:
                t_loc[at] = product
            else:
                t_loc[at] += product

    far = jnp.zeros((8, 128), F32)
    for s in range(ions // tile):
        lanes = pl.ds(s * tile, tile)
        block = ions_ref[:, lanes]
        base = base_tables(block)
        _, cx, sx, cy, sy, _, cz, sz = base
        tx_ref[0:32, lanes] = cx
        tx_ref[32:64, lanes] = sx
        ty_ref[0:32, lanes] = cy
        ty_ref[32:64, lanes] = sy
        tz_ref[0:8, lanes] = cz
        tz_ref[8:16, lanes] = sz
        build_b(cy, sy, cz, sz, b_hi, b_lo, lanes)
        build_a(0, block[3:4], jnp.concatenate([cx, sx], 0), cz, sz, a_hi, a_lo, lanes)
        turns = 32.0 * block[1:3]
        fc, fs = cos_sin(turns)
        four = jnp.concatenate([fc[0:1], fs[0:1], fc[1:2], fs[1:2]], 0)
        far_ref[0:4, lanes] = four
        value = jnp.concatenate([block[3:4] * four, jnp.zeros((4, tile), F32)], 0)
        for c in range(tile // 128):
            far += value[:, c * 128 : (c + 1) * 128]
        t_block(0, s, s + 1)

    ids = ids_ref[...]
    masks = mask_rows(ids)

    def patch(h):
        for k in range(16 * h, 16 * h + 16):
            t_loc[64 * (k // 4) + 32 : 64 * (k // 4) + 33, k % 4 * 128 : k % 4 * 128 + 128] = masks[k : k + 1]
        if h == 0:
            row = lax.broadcasted_iota(jnp.int32, (8, 128), 0)
            flags = far
            flags = jnp.where(row == 4, (ids == 32).astype(F32), flags)
            flags = jnp.where(row == 5, (ids == 2048).astype(F32), flags)
            lane = lax.broadcasted_iota(jnp.int32, (8, 128), 1)
            column = jnp.sum(flags, 1, keepdims=True)
            t_loc[0:8, 128:256] = jnp.where(lane == 0, column, t_loc[0:8, 128:256])

    def swap(h):
        theirs = pl.ds(pl.multiple_of(256 * h + 128 * (1 - core), 128), 128)
        return to_sibling(h, 0, t_loc.at[theirs], sib.at[h])

    def scatter(h):
        mine = pl.ds(pl.multiple_of(256 * h + 128 * core, 128), 128)
        own[h] = t_loc[mine] + sib[h]

        for step in ORDER:
            other = peer(me, step)
            r, l = tile_of(chip(other), 0)
            pltpu.make_async_remote_copy(
                src_ref=own.at[h, r, l],
                dst_ref=parts.at[h, step - 1],
                send_sem=sems.at[h, 2],
                recv_sem=sems.at[h, 3],
                device_id=device(*other),
                device_id_type=MESH,
            ).start()

    def gather(h):
        all_bytes(h, 3)
        r, l = tile_of(chip(me), 0)
        red[h] = own[h, r, l] + jnp.sum(parts[h], 0)
        where = tile_of(chip(me), 256 * h + 128 * core)
        full[where] = red[h]

        for step in ORDER:
            pltpu.make_async_remote_copy(
                src_ref=red.at[h],
                dst_ref=full.at[where],
                send_sem=sems.at[h, 4],
                recv_sem=sems.at[h, 5],
                device_id=device(*peer(me, step)),
                device_id_type=MESH,
            ).start()

    def forward(h):
        mine = full.at[pl.ds(pl.multiple_of(256 * h + 128 * core, 128), 128)]
        return to_sibling(h, 6, mine, mine)

    def small_tables():
        mx, _ = row_waves()
        units = A_UNIT / spread_a(mx), B_UNIT / spread_b(*row_waves())
        for s in range(ions // 128):
            lanes = pl.ds(s * 128, 128)
            for high, low, to, unit in ((a_hi, a_lo, a_8, units[0]), (b_hi, b_lo, b_8, units[1])):
                for k in range(0, NA, 128):
                    at = pl.ds(k, 128)
                    to[0, at, lanes] = (low[at, lanes].astype(F32) * (LOW * unit)).astype(F8)
                    to[1, at, lanes] = (high[at, lanes].astype(F32) * unit).astype(F8)

    def small(block, low, scale):
        return (block * scale).astype(F8), (low.astype(F32) * (scale * LOW)).astype(F8)

    def transpose(h, largest):
        largest = jnp.max(jnp.max(largest, 1, keepdims=True), 0, keepdims=True)
        scale = 128.0 / jnp.maximum(largest, 1e-30)
        a_rows, b_rows = spread_a(row_waves()[0]), spread_b(*row_waves())
        scale_d = scale * (a_rows * spread_b(*lane_waves()))
        scale_t = scale * (b_rows * spread_a(lane_waves()[0]))
        back = 1.0 / (scale * LOW)
        inv[0] = back / (B_UNIT * a_rows)
        inv[1] = back / (A_UNIT * b_rows)
        for i in (2 * h, 2 * h + 1):
            for j in range(NB // 128):
                block = d_ref[i * 128 : (i + 1) * 128, j * 128 : (j + 1) * 128]
                at = (pl.ds(i * 128, 128), pl.ds(j * 128, 128))
                high, low = split(block)
                d_hi[at] = high
                d_8[0, *at], d_8[1, *at] = small(block, low, scale_d)
                block = block.T
                at = (pl.ds(j * 128, 128), pl.ds(i * 128, 128))
                high, low = split(block)
                dt_hi[at] = high
                dt_8[0, *at], dt_8[1, *at] = small(block, low, scale_t)

    def z_rows(lanes, k):
        cz, sz = tz_ref[k : k + 1, lanes], tz_ref[8 + k : 9 + k, lanes]
        f = k + 0.5 if k < 4 else 8.0 * k - 28.5
        return (cz, sz), (-f * sz, f * cz)

    def force_a(h, lanes):
        at = pl.ds(h * 256, 256)
        h_a = jnp.dot(d_hi[at], b_hi[:, lanes], preferred_element_type=F32)
        cross = jnp.dot(
            jnp.concatenate([d_8[0, at], d_8[1, at]], 1),
            jnp.concatenate([b_8[0, :, lanes], b_8[1, :, lanes]], 0),
            preferred_element_type=F32,
        )
        h_a += jnp.concatenate([jnp.concatenate([inv[0]] * (tile2 // 128), 1)] * 2, 0) * cross
        v0 = vz = None
        for k in range(2):
            z, dz = z_rows(lanes, 2 * h + k)
            for cs in range(2):
                part = h_a[k * 128 + cs * 64 : k * 128 + cs * 64 + 64]
                v0 = z[cs] * part if v0 is None else v0 + z[cs] * part
                vz = dz[cs] * part if vz is None else vz + dz[cs] * part
        cx, sx = tx_ref[0:32, lanes], tx_ref[32:64, lanes]
        n = rows(32, tile2)
        phi = jnp.sum(cx * v0[:32] + sx * v0[32:], 0, keepdims=True)
        grad_x = jnp.sum(n * (cx * v0[32:] - sx * v0[:32]), 0, keepdims=True)
        grad_z = jnp.sum(cx * vz[:32] + sx * vz[32:], 0, keepdims=True)
        return phi, grad_x, grad_z

    def force_b(h, lanes):
        at = pl.ds(h * 256, 256)
        h_b = jnp.dot(dt_hi[:, at], a_hi[at, lanes], preferred_element_type=F32)
        cross = jnp.dot(
            jnp.concatenate([dt_8[0, :, at], dt_8[1, :, at]], 1),
            jnp.concatenate([a_8[0, at, lanes], a_8[1, at, lanes]], 0),
            preferred_element_type=F32,
        )
        h_b += jnp.concatenate([jnp.concatenate([inv[1]] * (tile2 // 128), 1)] * 4, 0) * cross
        u0, uz = [None, None], [None, None]
        for p in range(4):
            z, dz = z_rows(lanes, 4 + p)
            for cs in range(2):
                for ycs in range(2):
                    at = cs * 256 + ycs * 128 + p * 32
                    part = h_b[at : at + 32]
                    u0[ycs] = z[cs] * part if u0[ycs] is None else u0[ycs] + z[cs] * part
                    uz[ycs] = dz[cs] * part if uz[ycs] is None else uz[ycs] + dz[cs] * part
        cy, sy = ty_ref[0:32, lanes], ty_ref[32:64, lanes]
        n = rows(32, tile2)
        grad_y = jnp.sum(n * (cy * u0[1] - sy * u0[0]), 0, keepdims=True)
        grad_z = jnp.sum(cy * uz[0] + sy * uz[1], 0, keepdims=True)
        return grad_y, grad_z

    steps = ions // tile
    patch(0)
    pl.semaphore_wait(barrier, 64)
    swap0 = swap(0)
    swap0.start()
    t_block(1, 0, CUT)
    swap0.wait_recv()
    scatter(0)
    t_block(1, CUT, steps)
    patch(1)
    swap1 = swap(1)
    swap1.start()
    swap1.wait_recv()
    scatter(1)
    small_tables()
    gather(0)
    gather(1)
    all_bytes(0, 5)
    forward0 = forward(0)
    forward0.start()
    forward0.wait_recv()
    energy, largest = weights(0, full, d_ref)
    transpose(0, largest)
    forward1 = forward(1)
    steps2 = ions // tile2
    for s in range(steps2):
        lanes = pl.ds(s * tile2, tile2)
        if s == steps2 - LATE:
            all_bytes(1, 5)
            forward1.start()
        for k, value in enumerate(force_a(0, lanes) + force_b(0, lanes)):
            acc_ref[k : k + 1, lanes] = value
    forward1.wait_recv()
    more, largest = weights(1, full, d_ref)
    energy += more
    transpose(1, largest)

    copies = 1.0 / lax.axis_size("ion")
    column = full[0:8, 128:129]
    far_weight = 0.5 * math.exp(-1024.0 / 1600.0) / 1024.0
    wy = far_weight * copies * column[4:5]
    wz = far_weight * copies * column[5:6]
    fcy, fsy, fcz, fsz = wy * column[0:1], wy * column[1:2], wz * column[2:3], wz * column[3:4]
    energy = jnp.sum(jnp.sum(energy, 1, keepdims=True), 0, keepdims=True)
    energy += fcy * column[0:1] + fsy * column[1:2] + fcz * column[2:3] + fsz * column[3:4]
    energy_ref[...] = (0.01 / total) * energy
    force_scale = 0.04 * math.pi / math.sqrt(total)
    potential_scale = 0.4 / math.sqrt(total)

    for s in range(steps2):
        lanes = pl.ds(s * tile2, tile2)
        values = force_a(1, lanes) + force_b(1, lanes)
        phi, grad_x, grad_z, grad_y, grad_zb = (v + acc_ref[k : k + 1, lanes] for k, v in enumerate(values))
        charge = ions_ref[3:4, lanes]
        fcosy, fsiny, fcosz, fsinz = (far_ref[k : k + 1, lanes] for k in range(4))
        phi += fcy * fcosy + fsy * fsiny + fcz * fcosz + fsz * fsinz
        far_y = 32.0 * (fsy * fcosy - fcy * fsiny)
        far_z = 32.0 * (fsz * fcosz - fcz * fsinz)
        out_ref[0:1, lanes] = -force_scale * (charge * grad_x)
        out_ref[1:2, lanes] = -force_scale * (grad_y + charge * far_y)
        out_ref[2:3, lanes] = -force_scale * (grad_zb + charge * (grad_z + far_z))
        out_ref[3:4, lanes] = potential_scale * phi

    for h, (first, second) in enumerate(((swap0, forward0), (swap1, forward1))):
        first.wait_send()
        all_bytes(h, 2)
        all_bytes(h, 4)
        second.wait_send()


def per_device(ions, col_ids):
    count = ions.shape[1]
    total = count * lax.axis_size("kcol") * lax.axis_size("ion")
    forces, energy = pl.pallas_call(
        functools.partial(kernel, 512, 256, total),
        out_shape=(jax.ShapeDtypeStruct(ions.shape, F32), jax.ShapeDtypeStruct((1, 1), F32)),
        in_specs=[pl.BlockSpec(memory_space=pltpu.VMEM)] * 2,
        out_specs=[pl.BlockSpec(memory_space=pltpu.VMEM)] * 2,
        scratch_shapes=[
            pltpu.VMEM((64, count), F32),
            pltpu.VMEM((64, count), F32),
            pltpu.VMEM((16, count), F32),
            pltpu.VMEM((8, count), F32),
            pltpu.VMEM((8, count), F32),
            pltpu.VMEM((NA, count), BF16),
            pltpu.VMEM((NA, count), BF16),
            pltpu.VMEM((NB, count), BF16),
            pltpu.VMEM((NB, count), BF16),
            pltpu.VMEM((NA, NB), F32),
            pltpu.VMEM((2, 128, NB), F32),
            pltpu.VMEM((2, 128, NB), F32),
            pltpu.VMEM((2, 63, 8, 128), F32),
            pltpu.VMEM((2, 8, 128), F32),
            pltpu.VMEM((NA, NB), F32),
            pltpu.VMEM((NA, NB), F32),
            pltpu.VMEM((NA, NB), BF16),
            pltpu.VMEM((NB, NA), BF16),
            pltpu.VMEM((2, NA, count), F8),
            pltpu.VMEM((2, NB, count), F8),
            pltpu.VMEM((2, NA, NB), F8),
            pltpu.VMEM((2, NB, NA), F8),
            pltpu.VMEM((2, 128, 128), F32),
            pltpu.SemaphoreType.DMA((2, 8)),
        ],
        compiler_params=pltpu.CompilerParams(
            collective_id=0, has_side_effects=True, vmem_limit_bytes=VMEM_LIMIT
        ),
    )(ions, col_ids.reshape(1, -1))
    return forces, energy.reshape(())


def solution(mesh):
    return jax.shard_map(
        per_device,
        mesh=mesh,
        in_specs=(P(None, ("kcol", "ion")), P("kcol")),
        out_specs=(P(None, ("kcol", "ion")), P()),
        check_vma=False,
    )
```

```python
import functools
import math

import jax
import jax.numpy as jnp
from jax import lax
from jax.experimental import pallas as pl
from jax.experimental.pallas import tpu as pltpu
from jax.sharding import PartitionSpec as P

NA = 512
NB = 512
VMEM_LIMIT = 60 * 1024 * 1024
CUT = 1
LATE = 6
F32 = jnp.float32
BF16 = jnp.bfloat16
F8 = jnp.float8_e4m3fn
LOW = 1024.0
A_UNIT = 32.0
B_UNIT = 48.0
COS = [(-1.0) ** k / math.factorial(2 * k) for k in range(8)]
SIN = [(-1.0) ** k / math.factorial(2 * k + 1) for k in range(7)]


def cos_sin(turns):
    half = jnp.floor(2.0 * turns + 0.5)
    rest = turns - 0.5 * half
    sign = 1.0 - 4.0 * (0.5 * half - jnp.floor(0.5 * half))
    angle = (2.0 * math.pi) * rest
    square = angle * angle
    cosine = jnp.full_like(square, COS[-1])
    for c in COS[-2::-1]:
        cosine = cosine * square + c
    sine = jnp.full_like(square, SIN[-1])
    for c in SIN[-2::-1]:
        sine = sine * square + c
    return cosine * sign, sine * angle * sign


def rows(count, width):
    return lax.broadcasted_iota(jnp.int32, (count, width), 0).astype(F32)


def base_tables(block):
    width = block.shape[1]
    wave = rows(32, width)
    cx, sx = cos_sin(wave * block[0:1])
    cy, sy = cos_sin(wave * block[1:2])
    eight = rows(8, width)
    freq = jnp.where(eight < 4.0, eight + 0.5, 8.0 * eight - 28.5)
    cz, sz = cos_sin(freq * block[2:3])
    return wave, cx, sx, cy, sy, freq, cz, sz


def split(value):
    high = value.astype(BF16)
    low = (value - high.astype(F32)).astype(BF16)
    return high, low


def build_a(h, charge, tx, cz, sz, a_hi, a_lo, lanes):
    for r in (2 * h, 2 * h + 1):
        for cs, table in enumerate((cz, sz)):
            at = pl.ds(r * 128 + cs * 64, 64)
            high, low = split((charge * table[r : r + 1]) * tx)
            a_hi[at, lanes] = high
            a_lo[at, lanes] = low


def build_b(cy, sy, cz, sz, b_hi, b_lo, lanes):
    for cs, table in enumerate((cz, sz)):
        for ycs, ty in enumerate((cy, sy)):
            for p in range(4):
                at = pl.ds(cs * 256 + ycs * 128 + p * 32, 32)
                high, low = split(table[4 + p : 5 + p] * ty)
                b_hi[at, lanes] = high
                b_lo[at, lanes] = low


def dot_nt(a, b):
    return lax.dot_general(a, b, (((1,), (1,)), ((), ())), preferred_element_type=F32)


def mask_rows(ids):
    my = lax.shift_right_logical(ids, 6) - 32
    mz = (ids & 63) - 32
    ay, az = jnp.abs(my), jnp.abs(mz)
    low = az & 7
    plus = low >= 4
    r = jnp.where(plus, low - 4, 3 - low)
    row = r * 8 + jnp.where(plus, 0, 4) + jnp.where(my < 0, 2, 0) + jnp.where(mz < 0, 1, 0)
    lane = lax.shift_right_logical(az, 3) * 32 + ay
    row = jnp.where((ay > 31) | (az > 31), -1, row)
    count = ids.shape[1]
    left = (lax.broadcasted_iota(jnp.int32, (32, count), 0) == row).astype(F32).astype(BF16)
    right = (lax.broadcasted_iota(jnp.int32, (128, count), 0) == lane).astype(F32).astype(BF16)
    return dot_nt(left, right)


def spread_a(mx):
    return jnp.sqrt(mx * mx + 1.0)


def spread_b(my, p):
    mz = 8.0 * p + 3.5
    return jnp.sqrt(my * my + mz * mz)


def lane_waves():
    lane = lax.broadcasted_iota(jnp.int32, (128, 128), 1)
    return (lane & 31).astype(F32), lax.shift_right_logical(lane, 5).astype(F32)


def row_waves():
    row = lax.broadcasted_iota(jnp.int32, (128, 128), 0)
    return (row & 31).astype(F32), lax.shift_right_logical(row, 5).astype(F32)


def weights(h, t_ref, d_ref):
    lane = lax.broadcasted_iota(jnp.int32, (16, 128), 1)
    my = (lane & 31).astype(F32)
    p = lax.shift_right_logical(lane, 5).astype(F32)
    energy = jnp.zeros((16, 128), F32)
    largest = jnp.zeros((16, 128), F32)
    copies = 1.0 / lax.axis_size("ion")
    for r in (2 * h, 2 * h + 1):
        masks = [
            t_ref[r * 128 + k // 4 * 64 + 32 : r * 128 + k // 4 * 64 + 33, k % 4 * 128 : k % 4 * 128 + 128] * copies
            for k in range(8)
        ]
        for half in range(2):
            mx = rows(16, 128) + 16.0 * half
            even = spread_a(mx) * spread_b(my, p)
            tt = {}
            for zr in range(2):
                for x in range(2):
                    for zp in range(2):
                        for y in range(2):
                            tt[zr, x, zp, y] = t_ref[
                                pl.ds(r * 128 + zr * 64 + x * 32 + half * 16, 16),
                                pl.ds(zp * 256 + y * 128, 128),
                            ]
                            if x == 1 and half == 0:
                                tt[zr, x, zp, y] = jnp.where(mx == 0.0, 0.0, tt[zr, x, zp, y])
                            if (r, half, zr, x, zp, y) == (0, 0, 0, 0, 0, 1):
                                tt[zr, x, zp, y] = jnp.where(my == 0.0, 0.0, tt[zr, x, zp, y])
            dd = {}
            parts = {}
            for sgn in range(2):
                mz = 8.0 * p + (4.0 + r if sgn == 0 else 3.0 - r)
                m2 = mx * mx + my * my + mz * mz
                live = (m2 <= 1024.0) & (m2 > 0.0)
                h = jnp.where(mx == 0.0, 0.5, 1.0)
                w = jnp.where(live, h * jnp.exp(m2 * (-1.0 / 1600.0)) / jnp.maximum(m2, 1.0), 0.0)
                at = sgn * 4
                mpp, mpm, mmp, mmm = masks[at : at + 4]
                ws1, wd1 = w * (mpp + mmm), w * (mpp - mmm)
                ws2, wd2 = w * (mpm + mmp), w * (mpm - mmp)
                s = 1.0 if sgn == 0 else -1.0
                z = {}
                for x in range(2):
                    for y in range(2):
                        z[x, y, 0] = tt[0, x, 0, y] - s * tt[1, x, 1, y]
                        z[x, y, 1] = tt[0, x, 1, y] + s * tt[1, x, 0, y]
                um = [z[x, 0, 0] - z[x, 1, 1] for x in range(2)]
                up = [z[x, 0, 0] + z[x, 1, 1] for x in range(2)]
                vp = [z[x, 1, 0] + z[x, 0, 1] for x in range(2)]
                vm = [z[x, 1, 0] - z[x, 0, 1] for x in range(2)]
                um2 = [ws1 * um[0] - wd1 * vp[1], ws1 * um[1] + wd1 * vp[0]]
                vp2 = [ws1 * vp[0] + wd1 * um[1], ws1 * vp[1] - wd1 * um[0]]
                up2 = [ws2 * up[0] - wd2 * vm[1], ws2 * up[1] + wd2 * vm[0]]
                vm2 = [ws2 * vm[0] + wd2 * up[1], ws2 * vm[1] - wd2 * up[0]]
                for x in range(2):
                    energy += um[x] * um2[x] + vp[x] * vp2[x] + up[x] * up2[x] + vm[x] * vm2[x]
                    parts[sgn, x, 0, 0] = um2[x] + up2[x]
                    parts[sgn, x, 1, 1] = up2[x] - um2[x]
                    parts[sgn, x, 1, 0] = vp2[x] + vm2[x]
                    parts[sgn, x, 0, 1] = vp2[x] - vm2[x]
            for x in range(2):
                for y in range(2):
                    dd[0, x, 0, y] = parts[0, x, y, 0] + parts[1, x, y, 0]
                    dd[1, x, 1, y] = parts[1, x, y, 0] - parts[0, x, y, 0]
                    dd[0, x, 1, y] = parts[0, x, y, 1] + parts[1, x, y, 1]
                    dd[1, x, 0, y] = parts[0, x, y, 1] - parts[1, x, y, 1]
            for (zr, x, zp, y), value in dd.items():
                at = (pl.ds(r * 128 + zr * 64 + x * 32 + half * 16, 16), pl.ds(zp * 256 + y * 128, 128))
                d_ref[at] = value
                largest = jnp.maximum(largest, jnp.abs(value) * even)
    return energy, largest


MESH = pl.DeviceIdType.MESH


def hops(step):
    return sum(min(d, 4 - d) for d in (step >> 4, (step >> 2) & 3, step & 3))


ORDER = sorted(range(1, 64), key=lambda step: -hops(step))


def place():
    k, i = lax.axis_index("kcol"), lax.axis_index("ion")
    return i >> 1, k >> 2, (k & 2) | (i & 1), k & 1


def device(x, y, z, core):
    return {"kcol": (y << 2) | (z & 2) | core, "ion": (x << 1) | (z & 1)}


def peer(me, step):
    x, y, z, core = me
    return (x + (step >> 4)) & 3, (y + ((step >> 2) & 3)) & 3, (z + (step & 3)) & 3, core


def chip(where):
    return where[0] * 16 + where[1] * 4 + where[2]


def tile_of(index, row0):
    row = pl.multiple_of(row0 + (index >> 2) * 8, 8)
    return pl.ds(row, 8), pl.ds(pl.multiple_of((index & 3) * 128, 128), 128)


def kernel(
    tile,
    tile2,
    total,
    ions_hbm,
    ids_hbm,
    out_hbm,
    energy_ref,
    ions_ref,
    ids_ref,
    out_ref,
    local_sems,
    tx_ref,
    ty_ref,
    tz_ref,
    far_ref,
    acc_ref,
    a_hi,
    a_lo,
    b_hi,
    b_lo,
    t_loc,
    sib,
    own,
    parts,
    red,
    full,
    d_ref,
    d_hi,
    dt_hi,
    a_8,
    b_8,
    d_8,
    dt_8,
    inv,
    sems,
):
    ions = ions_ref.shape[1]
    load_ions = pltpu.make_async_copy(ions_hbm, ions_ref, local_sems.at[0])
    load_ids = pltpu.make_async_copy(ids_hbm, ids_ref, local_sems.at[1])
    load_ids.start()
    load_ions.start()
    me = place()
    core = me[3]
    sibling = device(me[0], me[1], me[2], 1 - core)
    barrier = pltpu.get_barrier_semaphore()

    for step in ORDER:
        pl.semaphore_signal(barrier, inc=1, device_id=device(*peer(me, step)), device_id_type=MESH)
    pl.semaphore_signal(barrier, inc=1, device_id=sibling, device_id_type=MESH)

    def to_sibling(h, k, src, dst):
        return pltpu.make_async_remote_copy(
            src_ref=src,
            dst_ref=dst,
            send_sem=sems.at[h, k],
            recv_sem=sems.at[h, k + 1],
            device_id=sibling,
            device_id_type=MESH,
        )

    def all_bytes(h, k):
        pltpu.make_async_copy(parts.at[h], parts.at[h], sems.at[h, k]).wait()

    wave = rows(32, tile)
    freq = rows(8, tile)
    freq = jnp.where(freq < 4.0, freq + 0.5, 8.0 * freq - 28.5)

    def t_block(h, first, last):
        for s in range(first, last):
            lanes = pl.ds(s * tile, tile)
            if h == 1:
                build_a(1, ions_ref[3:4, lanes], tx_ref[:, lanes], tz_ref[0:8, lanes], tz_ref[8:16, lanes], a_hi, a_lo, lanes)
            at = pl.ds(h * 256, 256)
            high = a_hi[at, lanes]
            left = jnp.concatenate([high, high, a_lo[at, lanes]], 1)
            right = jnp.concatenate([b_hi[:, lanes], b_lo[:, lanes], b_hi[:, lanes]], 1)
            product = dot_nt(left, right)
            if s == 0:
                t_loc[at] = product
            else:
                t_loc[at] += product

    load_ids.wait()
    ids = ids_ref[...]
    masks = mask_rows(ids)
    load_ions.wait()
    far = jnp.zeros((8, 128), F32)
    for s in range(ions // tile):
        lanes = pl.ds(s * tile, tile)
        block = ions_ref[:, lanes]
        base = base_tables(block)
        _, cx, sx, cy, sy, _, cz, sz = base
        tx_ref[0:32, lanes] = cx
        tx_ref[32:64, lanes] = sx
        ty_ref[0:32, lanes] = cy
        ty_ref[32:64, lanes] = sy
        tz_ref[0:8, lanes] = cz
        tz_ref[8:16, lanes] = sz
        build_b(cy, sy, cz, sz, b_hi, b_lo, lanes)
        build_a(0, block[3:4], jnp.concatenate([cx, sx], 0), cz, sz, a_hi, a_lo, lanes)
        turns = 32.0 * block[1:3]
        fc, fs = cos_sin(turns)
        four = jnp.concatenate([fc[0:1], fs[0:1], fc[1:2], fs[1:2]], 0)
        far_ref[0:4, lanes] = four
        value = jnp.concatenate([block[3:4] * four, jnp.zeros((4, tile), F32)], 0)
        for c in range(tile // 128):
            far += value[:, c * 128 : (c + 1) * 128]
        t_block(0, s, s + 1)

    def patch(h):
        for k in range(16 * h, 16 * h + 16):
            t_loc[64 * (k // 4) + 32 : 64 * (k // 4) + 33, k % 4 * 128 : k % 4 * 128 + 128] = masks[k : k + 1]
        if h == 0:
            row = lax.broadcasted_iota(jnp.int32, (8, 128), 0)
            flags = far
            flags = jnp.where(row == 4, (ids == 32).astype(F32), flags)
            flags = jnp.where(row == 5, (ids == 2048).astype(F32), flags)
            lane = lax.broadcasted_iota(jnp.int32, (8, 128), 1)
            column = jnp.sum(flags, 1, keepdims=True)
            t_loc[0:8, 128:256] = jnp.where(lane == 0, column, t_loc[0:8, 128:256])

    def swap(h):
        theirs = pl.ds(pl.multiple_of(256 * h + 128 * (1 - core), 128), 128)
        return to_sibling(h, 0, t_loc.at[theirs], sib.at[h])

    def scatter(h):
        mine = pl.ds(pl.multiple_of(256 * h + 128 * core, 128), 128)
        own[h] = t_loc[mine] + sib[h]

        for step in ORDER:
            other = peer(me, step)
            r, l = tile_of(chip(other), 0)
            pltpu.make_async_remote_copy(
                src_ref=own.at[h, r, l],
                dst_ref=parts.at[h, step - 1],
                send_sem=sems.at[h, 2],
                recv_sem=sems.at[h, 3],
                device_id=device(*other),
                device_id_type=MESH,
            ).start()

    def gather(h):
        all_bytes(h, 3)
        r, l = tile_of(chip(me), 0)
        sums = [jnp.sum(parts[h, k * 9 : k * 9 + 9], 0) for k in range(7)]
        red[h] = own[h, r, l] + ((sums[0] + sums[1]) + (sums[2] + sums[3])) + ((sums[4] + sums[5]) + sums[6])
        where = tile_of(chip(me), 256 * h + 128 * core)
        full[where] = red[h]

        for step in ORDER:
            pltpu.make_async_remote_copy(
                src_ref=red.at[h],
                dst_ref=full.at[where],
                send_sem=sems.at[h, 4],
                recv_sem=sems.at[h, 5],
                device_id=device(*peer(me, step)),
                device_id_type=MESH,
            ).start()

    def forward(h):
        mine = full.at[pl.ds(pl.multiple_of(256 * h + 128 * core, 128), 128)]
        return to_sibling(h, 6, mine, mine)

    def small_tables():
        mx, _ = row_waves()
        units = A_UNIT / spread_a(mx), B_UNIT / spread_b(*row_waves())
        for s in range(ions // 128):
            lanes = pl.ds(s * 128, 128)
            for high, low, to, unit in ((a_hi, a_lo, a_8, units[0]), (b_hi, b_lo, b_8, units[1])):
                for k in range(0, NA, 128):
                    at = pl.ds(k, 128)
                    to[0, at, lanes] = (low[at, lanes].astype(F32) * (LOW * unit)).astype(F8)
                    to[1, at, lanes] = (high[at, lanes].astype(F32) * unit).astype(F8)

    def small(block, low, scale):
        return (block * scale).astype(F8), (low.astype(F32) * (scale * LOW)).astype(F8)

    def transpose(h, largest):
        largest = jnp.max(jnp.max(largest, 1, keepdims=True), 0, keepdims=True)
        scale = 128.0 / jnp.maximum(largest, 1e-30)
        a_rows, b_rows = spread_a(row_waves()[0]), spread_b(*row_waves())
        scale_d = scale * (a_rows * spread_b(*lane_waves()))
        scale_t = scale * (b_rows * spread_a(lane_waves()[0]))
        back = 1.0 / (scale * LOW)
        inv[0] = back / (B_UNIT * a_rows)
        inv[1] = back / (A_UNIT * b_rows)
        for i in (2 * h, 2 * h + 1):
            for j in range(NB // 128):
                block = d_ref[i * 128 : (i + 1) * 128, j * 128 : (j + 1) * 128]
                at = (pl.ds(i * 128, 128), pl.ds(j * 128, 128))
                high, low = split(block)
                d_hi[at] = high
                d_8[0, *at], d_8[1, *at] = small(block, low, scale_d)
                block = block.T
                at = (pl.ds(j * 128, 128), pl.ds(i * 128, 128))
                high, low = split(block)
                dt_hi[at] = high
                dt_8[0, *at], dt_8[1, *at] = small(block, low, scale_t)

    def z_rows(lanes, k):
        cz, sz = tz_ref[k : k + 1, lanes], tz_ref[8 + k : 9 + k, lanes]
        f = k + 0.5 if k < 4 else 8.0 * k - 28.5
        return (cz, sz), (-f * sz, f * cz)

    def force_a(h, lanes):
        at = pl.ds(h * 256, 256)
        h_a = jnp.dot(d_hi[at], b_hi[:, lanes], preferred_element_type=F32)
        cross = jnp.dot(
            jnp.concatenate([d_8[0, at], d_8[1, at]], 1),
            jnp.concatenate([b_8[0, :, lanes], b_8[1, :, lanes]], 0),
            preferred_element_type=F32,
        )
        h_a += jnp.concatenate([jnp.concatenate([inv[0]] * (tile2 // 128), 1)] * 2, 0) * cross
        v0 = vz = None
        for k in range(2):
            z, dz = z_rows(lanes, 2 * h + k)
            for cs in range(2):
                part = h_a[k * 128 + cs * 64 : k * 128 + cs * 64 + 64]
                v0 = z[cs] * part if v0 is None else v0 + z[cs] * part
                vz = dz[cs] * part if vz is None else vz + dz[cs] * part
        cx, sx = tx_ref[0:32, lanes], tx_ref[32:64, lanes]
        n = rows(32, tile2)
        phi = jnp.sum(cx * v0[:32] + sx * v0[32:], 0, keepdims=True)
        grad_x = jnp.sum(n * (cx * v0[32:] - sx * v0[:32]), 0, keepdims=True)
        grad_z = jnp.sum(cx * vz[:32] + sx * vz[32:], 0, keepdims=True)
        return phi, grad_x, grad_z

    def force_b(h, lanes):
        at = pl.ds(h * 256, 256)
        h_b = jnp.dot(dt_hi[:, at], a_hi[at, lanes], preferred_element_type=F32)
        cross = jnp.dot(
            jnp.concatenate([dt_8[0, :, at], dt_8[1, :, at]], 1),
            jnp.concatenate([a_8[0, at, lanes], a_8[1, at, lanes]], 0),
            preferred_element_type=F32,
        )
        h_b += jnp.concatenate([jnp.concatenate([inv[1]] * (tile2 // 128), 1)] * 4, 0) * cross
        u0, uz = [None, None], [None, None]
        for p in range(4):
            z, dz = z_rows(lanes, 4 + p)
            for cs in range(2):
                for ycs in range(2):
                    at = cs * 256 + ycs * 128 + p * 32
                    part = h_b[at : at + 32]
                    u0[ycs] = z[cs] * part if u0[ycs] is None else u0[ycs] + z[cs] * part
                    uz[ycs] = dz[cs] * part if uz[ycs] is None else uz[ycs] + dz[cs] * part
        cy, sy = ty_ref[0:32, lanes], ty_ref[32:64, lanes]
        n = rows(32, tile2)
        grad_y = jnp.sum(n * (cy * u0[1] - sy * u0[0]), 0, keepdims=True)
        grad_z = jnp.sum(cy * uz[0] + sy * uz[1], 0, keepdims=True)
        return grad_y, grad_z

    steps = ions // tile
    patch(0)
    pl.semaphore_wait(barrier, 64)
    swap0 = swap(0)
    swap0.start()
    t_block(1, 0, CUT)
    swap0.wait_recv()
    scatter(0)
    t_block(1, CUT, steps)
    patch(1)
    swap1 = swap(1)
    swap1.start()
    swap1.wait_recv()
    scatter(1)
    small_tables()
    gather(0)
    gather(1)
    all_bytes(0, 5)
    forward0 = forward(0)
    forward0.start()
    forward0.wait_recv()
    energy, largest = weights(0, full, d_ref)
    transpose(0, largest)
    forward1 = forward(1)
    steps2 = ions // tile2
    for s in range(steps2):
        lanes = pl.ds(s * tile2, tile2)
        if s == steps2 - LATE:
            all_bytes(1, 5)
            forward1.start()
        for k, value in enumerate(force_a(0, lanes) + force_b(0, lanes)):
            acc_ref[k : k + 1, lanes] = value
    forward1.wait_recv()
    more, largest = weights(1, full, d_ref)
    energy += more
    transpose(1, largest)

    copies = 1.0 / lax.axis_size("ion")
    column = full[0:8, 128:129]
    far_weight = 0.5 * math.exp(-1024.0 / 1600.0) / 1024.0
    wy = far_weight * copies * column[4:5]
    wz = far_weight * copies * column[5:6]
    fcy, fsy, fcz, fsz = wy * column[0:1], wy * column[1:2], wz * column[2:3], wz * column[3:4]
    energy = jnp.sum(jnp.sum(energy, 1, keepdims=True), 0, keepdims=True)
    energy += fcy * column[0:1] + fsy * column[1:2] + fcz * column[2:3] + fsz * column[3:4]
    energy_ref[...] = (0.01 / total) * energy
    force_scale = 0.04 * math.pi / math.sqrt(total)
    potential_scale = 0.4 / math.sqrt(total)

    def store(k):
        lanes = pl.ds(k * (ions // 2), ions // 2)
        return pltpu.make_async_copy(out_ref.at[:, lanes], out_hbm.at[:, lanes], local_sems.at[2 + k])

    for s in range(steps2):
        lanes = pl.ds(s * tile2, tile2)
        values = force_a(1, lanes) + force_b(1, lanes)
        phi, grad_x, grad_z, grad_y, grad_zb = (v + acc_ref[k : k + 1, lanes] for k, v in enumerate(values))
        charge = ions_ref[3:4, lanes]
        fcosy, fsiny, fcosz, fsinz = (far_ref[k : k + 1, lanes] for k in range(4))
        phi += fcy * fcosy + fsy * fsiny + fcz * fcosz + fsz * fsinz
        far_y = 32.0 * (fsy * fcosy - fcy * fsiny)
        far_z = 32.0 * (fsz * fcosz - fcz * fsinz)
        out_ref[0:1, lanes] = -force_scale * (charge * grad_x)
        out_ref[1:2, lanes] = -force_scale * (grad_y + charge * far_y)
        out_ref[2:3, lanes] = -force_scale * (grad_zb + charge * (grad_z + far_z))
        out_ref[3:4, lanes] = potential_scale * phi
        if s == steps2 // 2 - 1:
            store(0).start()
    store(1).start()

    for h, (first, second) in enumerate(((swap0, forward0), (swap1, forward1))):
        first.wait_send()
        all_bytes(h, 2)
        all_bytes(h, 4)
        second.wait_send()
    store(0).wait()
    store(1).wait()


def per_device(ions, col_ids):
    count = ions.shape[1]
    total = count * lax.axis_size("kcol") * lax.axis_size("ion")
    forces, energy = pl.pallas_call(
        functools.partial(kernel, 512, 256, total),
        out_shape=(jax.ShapeDtypeStruct(ions.shape, F32), jax.ShapeDtypeStruct((1, 1), F32)),
        in_specs=[pl.BlockSpec(memory_space=pl.ANY)] * 2,
        out_specs=[pl.BlockSpec(memory_space=pl.ANY), pl.BlockSpec(memory_space=pltpu.VMEM)],
        scratch_shapes=[
            pltpu.VMEM((4, count), F32),
            pltpu.VMEM((1, col_ids.shape[0]), jnp.int32),
            pltpu.VMEM((4, count), F32),
            pltpu.SemaphoreType.DMA((4,)),
            pltpu.VMEM((64, count), F32),
            pltpu.VMEM((64, count), F32),
            pltpu.VMEM((16, count), F32),
            pltpu.VMEM((8, count), F32),
            pltpu.VMEM((8, count), F32),
            pltpu.VMEM((NA, count), BF16),
            pltpu.VMEM((NA, count), BF16),
            pltpu.VMEM((NB, count), BF16),
            pltpu.VMEM((NB, count), BF16),
            pltpu.VMEM((NA, NB), F32),
            pltpu.VMEM((2, 128, NB), F32),
            pltpu.VMEM((2, 128, NB), F32),
            pltpu.VMEM((2, 63, 8, 128), F32),
            pltpu.VMEM((2, 8, 128), F32),
            pltpu.VMEM((NA, NB), F32),
            pltpu.VMEM((NA, NB), F32),
            pltpu.VMEM((NA, NB), BF16),
            pltpu.VMEM((NB, NA), BF16),
            pltpu.VMEM((2, NA, count), F8),
            pltpu.VMEM((2, NB, count), F8),
            pltpu.VMEM((2, NA, NB), F8),
            pltpu.VMEM((2, NB, NA), F8),
            pltpu.VMEM((2, 128, 128), F32),
            pltpu.SemaphoreType.DMA((2, 8)),
        ],
        compiler_params=pltpu.CompilerParams(
            collective_id=0, has_side_effects=True, vmem_limit_bytes=VMEM_LIMIT
        ),
    )(ions, col_ids.reshape(1, -1))
    return forces, energy.reshape(())


def solution(mesh):
    return jax.shard_map(
        per_device,
        mesh=mesh,
        in_specs=(P(None, ("kcol", "ion")), P("kcol")),
        out_specs=(P(None, ("kcol", "ion")), P()),
        check_vma=False,
    )
```
